32 devices in a mesh: section: 4 (over z), expert: 4 (over y, x), dp: 2 (over core).
Axes of the slice: x: 2, y: 2, z: 4, core: 2. Of those that a mesh axis runs over, the one named last changes fastest.
Arguments:
- acts: bfloat16 [4, 3, 512, 1024], P('section', None, ('expert', 'dp')), may hold values from -6 to 6
- out_grad: bfloat16 [3, 512, 1024], P(None, ('expert', 'dp')), may hold values from -6 to 6
- ln_gain: float32 [4, 1024], P('section'), may hold values from 0.1 to 1.9
- router: bfloat16 [4, 1024, 4], P('section'), may hold values from -0.1875 to 0.1875
- w_in: bfloat16 [4, 4, 1024, 4096], P('section', 'expert', None, 'dp'), may hold values from -0.1875 to 0.1875
- w_out: bfloat16 [4, 4, 4096, 1024], P('section', 'expert', 'dp'), may hold values from -0.09375 to 0.09375
- expert_ids: int32 [4, 3, 512, 2], P('section', None, ('expert', 'dp')), may hold values from 0 to 3, as said below
- slot_ids: int32 [4, 3, 512, 2], P('section', None, ('expert', 'dp')), may hold values from 0 to 39, as said below
- capacity: int32 [4, 3, 4], P('section'), may hold values from 20 to 40
Outputs:
- in_grads: bfloat16 [4, 3, 512, 1024], P('section', None, ('expert', 'dp'))
- gain_grad: float32 [4, 1024], P('section')
- router_grad: float32 [4, 1024, 4], P('section')
The draws below stay inside these ranges and needn't reach their ends.
Inputs may be any that keep to these rules, and one draw needn't show every extreme that they name: `expert_ids`: A token's two experts differ. `slot_ids`: within one block, micro-batch and aligned block of 64 tokens (the tokens of one device), the choices that name one expert hold the slots 0, 1, 2, ... without gaps, at most 40 of them; in every block and micro-batch one expert has 40 choices from every aligned block and capacity 40.
All inputs are finite; a program needn't handle non-finite values.
Results may differ from the reference program's by a relative error of at most 0.03.
Values may be sent and summed in bfloat16 or wider, within the bound.
No kernel may reach another device: no remote copies, remote signals or barrier semaphores. Data moves between devices by JAX's collectives and lax.ppermute only.
A program may use at most 128 MiB of HBM per device.

```python
import math
import jax
import jax.numpy as jnp
from jax import lax

D = 1024
H = 4096
TOP = 2
MB = 3
TOK_DEV = 64
SECTIONS = 4
EXPERTS = 4
TOKENS = 512
CAP = 40


def route_tables(key):
    base_key = jax.random.fold_in(key, 1001)
    key_full, key_cap, key_order, key_tok, key_limit = jax.random.split(base_key, 5)
    block_count = TOKENS // TOK_DEV
    columns = jnp.arange(EXPERTS, dtype=jnp.int32)
    full_expert = jax.random.randint(key_full, (SECTIONS, MB), 0, EXPERTS, dtype=jnp.int32)
    is_full = columns[None, None, None, :] == full_expert[:, :, None, None]
    lower_cap = CAP - CAP // 5
    load_caps = jax.random.randint(key_cap, (SECTIONS, MB, block_count, EXPERTS), lower_cap, CAP + 1, dtype=jnp.int32)
    load_caps = jnp.where(is_full, CAP, load_caps)
    order_score = jax.random.randint(key_order, (SECTIONS, MB, block_count, EXPERTS), 0, 1 << 20, dtype=jnp.int32) * EXPERTS + columns
    order_score = jnp.where(is_full, -1, order_score)
    expert_order = jnp.argsort(order_score, axis=-1, stable=True).astype(jnp.int32)
    ordered_caps = jnp.take_along_axis(load_caps, expert_order, axis=-1)
    load_ends = jnp.cumsum(ordered_caps, axis=-1)
    load_starts = load_ends - ordered_caps
    total_choices = TOP * TOK_DEV
    load_used = jnp.clip(total_choices - load_starts, 0, ordered_caps)
    used_ends = jnp.cumsum(load_used, axis=-1)
    used_starts = used_ends - load_used
    layout = jnp.arange(total_choices, dtype=jnp.int32)
    group_index = jnp.sum((used_ends[..., None, :] <= layout[:, None]).astype(jnp.int32), axis=-1)
    expert_at = jnp.take_along_axis(expert_order, group_index, axis=-1)
    slot_at = layout - jnp.take_along_axis(used_starts, group_index, axis=-1)
    token_score = jax.random.randint(key_tok, (SECTIONS, MB, block_count, TOK_DEV), 0, 1 << 20, dtype=jnp.int32) * TOK_DEV + jnp.arange(TOK_DEV, dtype=jnp.int32)
    token_perm = jnp.argsort(token_score, axis=-1, stable=True).astype(jnp.int32)
    token_place = jnp.argsort(token_perm, axis=-1, stable=True).astype(jnp.int32)
    layout_index = token_place[..., None] + jnp.arange(TOP, dtype=jnp.int32) * TOK_DEV
    layout_flat = layout_index.reshape(SECTIONS, MB, block_count, TOK_DEV * TOP)
    selected_expert_index = jnp.take_along_axis(expert_at, layout_flat, axis=-1).reshape(SECTIONS, MB, TOKENS, TOP)
    chosen_slots = jnp.take_along_axis(slot_at, layout_flat, axis=-1).reshape(SECTIONS, MB, TOKENS, TOP)
    limits = jax.random.randint(key_limit, (SECTIONS, MB, EXPERTS), CAP // 2, CAP + 1, dtype=jnp.int32)
    limits = jnp.where(columns[None, None, :] == full_expert[:, :, None], CAP, limits)
    return (selected_expert_index.astype(jnp.int32), chosen_slots.astype(jnp.int32), limits.astype(jnp.int32))


def draw_expert_ids(key, part):
    return route_tables(key)[0]


def draw_slot_ids(key, part):
    return route_tables(key)[1]


def draw_capacity(key, part):
    return route_tables(key)[2]


def steps_of(stream_key, extent, cuts, least, largest):
    def one(axis_at, blocks):
        heights = jax.random.uniform(jax.random.fold_in(jax.random.fold_in(stream_key, 6), axis_at), (blocks,), jnp.float32, least / len(cuts), largest / len(cuts))
        return jnp.repeat(jnp.exp(heights), extent[axis_at] // blocks).reshape((-1,) + (1,) * (len(extent) - axis_at - 1))

    level = one(*cuts[0])
    for cut in cuts[1:]:
        level = level * one(*cut)
    return level


def normal_values(own_key, dims, scale, most, cuts=(), held_as=jnp.bfloat16):
    drawn = scale * jax.random.normal(own_key, dims, jnp.float32)
    if cuts:
        drawn = drawn * steps_of(own_key, dims, cuts, -0.22, 0.18)
    return jnp.clip(drawn, -most, most).astype(held_as)


def setup_inputs(seed: int = 0) -> dict:
    key_list = jax.random.split(jax.random.key(seed), 10)
    return {
        "acts": normal_values(key_list[0], (SECTIONS, MB, TOKENS, D), 1.0, 6.0, ((0, 4), (2, 8))),
        "out_grad": normal_values(key_list[1], (MB, TOKENS, D), 1.0, 6.0, ((1, 8),)),
        "ln_gain": jnp.clip(1.0 + 0.18 * jax.random.normal(key_list[2], (SECTIONS, D), jnp.float32), 0.1, 1.9),
        "router": normal_values(key_list[3], (SECTIONS, D, EXPERTS), D ** -0.5, 0.1875, ((0, 4),)),
        "w_in": normal_values(key_list[4], (SECTIONS, EXPERTS, D, H), D ** -0.5, 0.1875, ((0, 4), (1, 4), (3, 2))),
        "w_out": normal_values(key_list[5], (SECTIONS, EXPERTS, H, D), H ** -0.5, 0.09375, ((0, 4), (1, 4), (2, 2))),
        "expert_ids": draw_expert_ids(jax.random.fold_in(key_list[9], 71), 0),
        "slot_ids": draw_slot_ids(jax.random.fold_in(key_list[9], 71), 0),
        "capacity": draw_capacity(jax.random.fold_in(key_list[9], 71), 0),
    }


GELU_C = math.sqrt(2.0 / math.pi)
PRECISE = lax.Precision.HIGHEST

def gelu_pair(hidden):
    inner_arg = GELU_C * (hidden + 0.044715 * hidden * hidden * hidden)
    tanh_val = jnp.tanh(inner_arg)
    active = 0.5 * hidden * (1.0 + tanh_val)
    gelu_slope = 0.5 * (1.0 + tanh_val) + 0.5 * hidden * (1.0 - tanh_val * tanh_val) * GELU_C * (1.0 + 3.0 * 0.044715 * hidden * hidden)
    return (active, gelu_slope)

def token_forward(inputs, norm_scale_weight, router_w):
    values = inputs.astype(jnp.float32)
    centred = values - lax.optimization_barrier(jnp.mean(values, axis=-1, keepdims=True))
    inverse_deviation = lax.rsqrt(lax.optimization_barrier(jnp.mean(centred * centred, axis=-1, keepdims=True)) + 1e-06)
    expert_unit_rows = centred * inverse_deviation
    normed = (expert_unit_rows * norm_scale_weight).astype(jnp.bfloat16)
    logits = jnp.dot(normed, router_w, preferred_element_type=jnp.float32)
    return (expert_unit_rows, inverse_deviation, normed, logits)

def gate_pair(chosen):
    first_gate = 1.0 / (1.0 + jnp.exp(chosen[:, 1] - chosen[:, 0]))
    return jnp.stack([first_gate, 1.0 - first_gate], axis=1)

def token_backward(grad_out, expert_unit_rows, inverse_deviation, normed, norm_scale_weight, router_w, gate_vals, pick_table, gate_dots, expert_part):
    gate_diff = gate_vals[:, 0] * gate_vals[:, 1] * (gate_dots[:, 0] - gate_dots[:, 1])
    dlogits = gate_diff[:, None] * (pick_table[:, 0, :] - pick_table[:, 1, :])
    norm_gradient = expert_part + jnp.dot(dlogits, router_w.astype(jnp.float32).T, precision=PRECISE)
    router_term = jnp.dot(normed.astype(jnp.float32).T, dlogits, precision=PRECISE)
    gain_term = lax.optimization_barrier(jnp.sum(norm_gradient * expert_unit_rows, axis=0))
    normalized_input_gradient = norm_gradient * norm_scale_weight
    input_gradient = inverse_deviation * (normalized_input_gradient - lax.optimization_barrier(jnp.mean(normalized_input_gradient, axis=-1, keepdims=True)) - expert_unit_rows * lax.optimization_barrier(jnp.mean(normalized_input_gradient * expert_unit_rows, axis=-1, keepdims=True)))
    in_grad = (grad_out.astype(jnp.float32) + input_gradient).astype(jnp.bfloat16)
    return (in_grad, gain_term, router_term)

def expert_backward(rows_u, rows_grad, first_proj, second_proj):
    hidden = jnp.dot(rows_u, first_proj, preferred_element_type=jnp.float32)
    active, gelu_slope = gelu_pair(hidden)
    back_grad = jnp.dot(rows_grad, second_proj.T, preferred_element_type=jnp.float32)
    gate_dot = lax.optimization_barrier(jnp.sum(active * back_grad, axis=-1)).astype(jnp.bfloat16)
    pre_grad = (back_grad * gelu_slope).astype(jnp.bfloat16)
    slot_grad = jnp.dot(pre_grad, first_proj.T, preferred_element_type=jnp.float32).astype(jnp.bfloat16)
    return (slot_grad, gate_dot)

def reference(acts, out_grad, ln_gain, router, w_in, w_out, expert_ids, slot_ids, capacity):
    block_count = TOKENS // TOK_DEV
    dump_row = block_count * EXPERTS * CAP
    block_of = jnp.arange(TOKENS, dtype=jnp.int32) // TOK_DEV
    columns = jnp.arange(EXPERTS, dtype=jnp.int32)
    grad_scale = 1.0 / math.sqrt(MB * TOKENS)
    incoming = [out_grad[micro_index] for micro_index in range(MB)]
    grads_all = [None] * SECTIONS
    gains_all = [None] * SECTIONS
    routers_all = [None] * SECTIONS
    for section_index in range(SECTIONS - 1, -1, -1):
        gain_sum = jnp.zeros((D,), jnp.float32)
        router_sum = jnp.zeros((D, EXPERTS), jnp.float32)
        outgoing = []
        for micro_index in range(MB):
            grad_out = incoming[micro_index]
            selected_expert_index = expert_ids[section_index, micro_index]
            chosen_slots = slot_ids[section_index, micro_index]
            expert_unit_rows, inverse_deviation, normed, logits = token_forward(acts[section_index, micro_index], ln_gain[section_index], router[section_index])
            gate_vals = gate_pair(jnp.take_along_axis(logits, selected_expert_index, axis=1))
            kept_mask = chosen_slots < capacity[section_index, micro_index][selected_expert_index]
            flat_index = jnp.where(kept_mask, (block_of[:, None] * EXPERTS + selected_expert_index) * CAP + chosen_slots, dump_row).astype(jnp.int32)
            flat_list = flat_index.reshape(-1)
            rows_u = jnp.zeros((dump_row + 1, D), jnp.bfloat16).at[flat_list].set(jnp.repeat(normed, TOP, axis=0))[:dump_row]
            rows_grad = jnp.zeros((dump_row + 1, D), jnp.bfloat16).at[flat_list].set(jnp.repeat(grad_out, TOP, axis=0))[:dump_row]
            rows_u = rows_u.reshape(block_count, EXPERTS, CAP, D).transpose(1, 0, 2, 3).reshape(EXPERTS, block_count * CAP, D)
            rows_grad = rows_grad.reshape(block_count, EXPERTS, CAP, D).transpose(1, 0, 2, 3).reshape(EXPERTS, block_count * CAP, D)
            slot_grad, gate_dot = lax.map(lambda packed: expert_backward(packed[0], packed[1], packed[2], packed[3]), (rows_u, rows_grad, w_in[section_index], w_out[section_index]))
            slot_grad = slot_grad.reshape(EXPERTS, block_count, CAP, D).transpose(1, 0, 2, 3).reshape(dump_row, D)
            gate_dot = gate_dot.reshape(EXPERTS, block_count, CAP).transpose(1, 0, 2).reshape(dump_row)
            slot_grad = jnp.concatenate([slot_grad, jnp.zeros((1, D), jnp.bfloat16)], axis=0)
            gate_dot = jnp.concatenate([gate_dot, jnp.zeros((1,), jnp.bfloat16)], axis=0)
            picked_rows = slot_grad[flat_index].astype(jnp.float32)
            expert_part = lax.optimization_barrier(jnp.sum(gate_vals[:, :, None] * picked_rows, axis=1))
            gate_dots = gate_dot[flat_index].astype(jnp.float32)
            pick_table = (selected_expert_index[:, :, None] == columns).astype(jnp.float32)
            in_grad, gain_term, router_term = token_backward(grad_out, expert_unit_rows, inverse_deviation, normed, ln_gain[section_index], router[section_index], gate_vals, pick_table, gate_dots, expert_part)
            outgoing.append(in_grad)
            gain_sum = gain_sum + gain_term
            router_sum = router_sum + router_term
        grads_all[section_index] = jnp.stack(outgoing)
        gains_all[section_index] = gain_sum * grad_scale
        routers_all[section_index] = router_sum * grad_scale
        incoming = outgoing
    return (jnp.stack(grads_all), jnp.stack(gains_all), jnp.stack(routers_all))
```

```python
import functools
import math

import jax
import jax.numpy as jnp
from jax import lax
from jax.experimental import pallas as pl
from jax.experimental.pallas import tpu as pltpu
from jax.sharding import PartitionSpec as P

GELU_C = math.sqrt(2.0 / math.pi)
LANES = 128
VMEM_BYTES = 40 * 1024 * 1024
F32 = jnp.float32
BF16 = jnp.bfloat16
NT = (((1,), (1,)), ((), ()))
TN = (((0,), (0,)), ((), ()))


def peers(count):
    if count & (count - 1) == 0:
        return [[(i, i ^ j) for i in range(count)] for j in range(1, count)]
    return [[(i, (i + j) % count) for i in range(count)] for j in range(1, count)]


def relative(ids, me, count):
    if count & (count - 1) == 0:
        return jnp.bitwise_xor(ids, me)
    return jnp.remainder(ids - me + count, count)


def exchange(chunks, back=False):
    count = len(chunks)
    out = [chunks[0]]
    for j, pairs in enumerate(peers(count), 1):
        moved = [(b, a) for a, b in pairs] if back else pairs
        out.append(lax.ppermute(chunks[j], "expert", moved))
    return out


def split_hi_lo(values):
    hi = values.astype(BF16)
    return hi, (values - hi.astype(F32)).astype(BF16)


def hidden_kernel(pick_ref, u_ref, *refs, halves, steps, width):
    first_refs, (active_ref, slope_ref) = refs[:halves], refs[halves:]
    step = pl.program_id(0)
    for half in range(halves):

        @pl.when(step // steps == half)
        def _(half=half):
            hidden = jnp.dot(
                u_ref[0, :, :width], first_refs[half][...], preferred_element_type=F32
            )
            square = hidden * hidden
            tanh_val = jnp.tanh(GELU_C * hidden * (1.0 + 0.044715 * square))
            up = 0.5 * (1.0 + tanh_val)
            active_ref[...] = (hidden * up).astype(BF16)
            rise = (GELU_C * hidden) * (1.0 + 3.0 * 0.044715 * square)
            slope_ref[...] = (up * (1.0 + (1.0 - tanh_val) * rise)).astype(BF16)


def half_spec(shape, axis, half, steps):
    def place(i, *_):
        at = jnp.clip(i - half * steps, 0, steps - 1)
        return (at, 0) if axis == 0 else (0, at)

    return pl.BlockSpec(shape, place)


def run_hidden(pick, stack, first_parts, tile):
    rows, packed = stack.shape[1], stack.shape[2]
    width, part = first_parts[0].shape
    halves, steps = len(first_parts), part // tile
    out = jax.ShapeDtypeStruct((rows, halves * part), BF16)
    return pl.pallas_call(
        functools.partial(hidden_kernel, halves=halves, steps=steps, width=width),
        grid_spec=pltpu.PrefetchScalarGridSpec(
            num_scalar_prefetch=1,
            grid=(halves * steps,),
            in_specs=[pl.BlockSpec((1, rows, packed), lambda i, pick: (pick[0], 0, 0))]
            + [half_spec((width, tile), 1, half, steps) for half in range(halves)],
            out_specs=[pl.BlockSpec((rows, tile), lambda i, pick: (0, i))] * 2,
        ),
        out_shape=[out, out],
        compiler_params=pltpu.CompilerParams(vmem_limit_bytes=VMEM_BYTES),
        cost_estimate=pl.CostEstimate(
            flops=2 * rows * width * halves * part,
            bytes_accessed=2 * width * halves * part,
            transcendentals=rows * halves * part,
        ),
        name="hidden",
    )(pick, stack, *first_parts)


def expert_kernel(pick_ref, u_ref, grad_ref, active_ref, slope_ref, *refs, halves, steps, width, experts):
    first_refs, second_refs = refs[:halves], refs[halves : 2 * halves]
    router_ref, gain_ref, sums_in_ref, out_ref, sums_ref, slot_acc, gate_acc = refs[2 * halves :]
    step = pl.program_id(0)

    @pl.when(step == 0)
    def _():
        slot_acc[...] = jnp.zeros_like(slot_acc)
        gate_acc[...] = jnp.zeros_like(gate_acc)

    for half in range(halves):

        @pl.when(step // steps == half)
        def _(half=half):
            back = lax.dot_general(
                grad_ref[...], second_refs[half][...], NT, preferred_element_type=F32
            )
            product = active_ref[...].astype(F32) * back
            folded = product[:, :LANES]
            for at in range(LANES, product.shape[1], LANES):
                folded = folded + product[:, at : at + LANES]
            gate_acc[...] += folded
            pre = (back * slope_ref[...].astype(F32)).astype(BF16)
            slot_acc[...] += lax.dot_general(
                pre, first_refs[half][...], NT, preferred_element_type=F32
            )

    @pl.when(step == halves * steps - 1)
    def _():
        meta = u_ref[0, :, width:].astype(F32)
        unit_gain = u_ref[0, :, :width]
        gate = meta[:, experts : experts + 1] + meta[:, experts + 1 : experts + 2]
        both = meta[:, experts + 2 : experts + 3] + meta[:, experts + 3 : experts + 4]
        dots = jnp.sum(gate_acc[...], axis=1, keepdims=True)
        lane = lax.broadcasted_iota(jnp.int32, meta.shape, 1)
        dlogits = jnp.where(lane < experts, meta, 0.0) * (both * dots)
        high, low = split_hi_lo(dlogits)
        router_rows = jnp.dot(high, router_ref[...], preferred_element_type=F32) + jnp.dot(
            low, router_ref[...], preferred_element_type=F32
        )
        result = gate * slot_acc[...] + router_rows
        out_ref[...] = result.astype(BF16)
        gain_part = jnp.sum(result * unit_gain.astype(F32), axis=0, keepdims=True) / gain_ref[...]
        router_part = lax.dot_general(high, unit_gain, TN, preferred_element_type=F32)
        sums_ref[:8, :] = sums_in_ref[:8, :] + jnp.broadcast_to(gain_part, (8, width))
        sums_ref[8:, :] = sums_in_ref[8:, :] + router_part[: sums_ref.shape[0] - 8, :]


def run_experts(pick, stack, grad_rows, active, slope, first_parts, second_parts, router_pad, gain, sums, experts, tile):
    rows, packed = stack.shape[1], stack.shape[2]
    width, part = first_parts[0].shape
    halves, steps = len(first_parts), part // tile

    def whole(shape):
        return pl.BlockSpec(shape, lambda i, pick: (0,) * len(shape))

    return pl.pallas_call(
        functools.partial(expert_kernel, halves=halves, steps=steps, width=width, experts=experts),
        grid_spec=pltpu.PrefetchScalarGridSpec(
            num_scalar_prefetch=1,
            grid=(halves * steps,),
            in_specs=[
                pl.BlockSpec((1, rows, packed), lambda i, pick: (pick[0], 0, 0)),
                whole((rows, width)),
                pl.BlockSpec((rows, tile), lambda i, pick: (0, i)),
                pl.BlockSpec((rows, tile), lambda i, pick: (0, i)),
            ]
            + [half_spec((width, tile), 1, half, steps) for half in range(halves)]
            + [half_spec((tile, width), 0, half, steps) for half in range(halves)]
            + [whole(router_pad.shape), whole(gain.shape), whole(sums.shape)],
            out_specs=[whole((rows, width)), whole(sums.shape)],
            scratch_shapes=[pltpu.VMEM((rows, width), F32), pltpu.VMEM((rows, LANES), F32)],
        ),
        out_shape=[
            jax.ShapeDtypeStruct((rows, width), BF16),
            jax.ShapeDtypeStruct(sums.shape, F32),
        ],
        compiler_params=pltpu.CompilerParams(vmem_limit_bytes=VMEM_BYTES),
        cost_estimate=pl.CostEstimate(
            flops=4 * rows * width * halves * part,
            bytes_accessed=4 * width * halves * part,
            transcendentals=0,
        ),
        name="expert",
    )(pick, stack, grad_rows, active, slope, *first_parts, *second_parts, router_pad, gain, sums)


def token_kernel(pick_ref, acts_ref, gain_ref, target_ref, ret_ref, grad_ref, out_ref):
    pick = pick_ref[0]
    values = acts_ref[pick].astype(F32)
    centred = values - jnp.mean(values, axis=-1, keepdims=True)
    inverse = lax.rsqrt(jnp.mean(centred * centred, axis=-1, keepdims=True) + 1e-06)
    unit = centred * inverse
    target = target_ref[pick]
    place = lax.broadcasted_iota(jnp.int32, (values.shape[0], ret_ref.shape[0]), 1)
    hit = jnp.logical_or(place == target[:, 0:1], place == target[:, 1:2])
    norm_grad = jnp.dot(
        jnp.where(hit, 1.0, 0.0).astype(BF16), ret_ref[...], preferred_element_type=F32
    )
    scaled = norm_grad * gain_ref[...]
    change = inverse * (
        scaled
        - jnp.mean(scaled, axis=-1, keepdims=True)
        - unit * jnp.mean(scaled * unit, axis=-1, keepdims=True)
    )
    out_ref[...] = (grad_ref[...].astype(F32) + change).astype(BF16)


def run_tokens(pick, acts, gain, target, ret, grad):
    smem = pl.BlockSpec(memory_space=pltpu.SMEM)
    vmem = pl.BlockSpec(memory_space=pltpu.VMEM)
    return pl.pallas_call(
        token_kernel,
        in_specs=[smem] + [vmem] * 5,
        out_specs=vmem,
        out_shape=jax.ShapeDtypeStruct(grad.shape, BF16),
        name="token",
    )(pick, acts, gain, target, ret, grad)


def rows_kernel(pick_ref, target_ref, in_ref, last_ref, grad_ref, rows_ref):
    pick = pick_ref[0]
    grad = jnp.where(pick_ref[1] > 0, last_ref[pick], in_ref[...])
    grad_ref[...] = grad
    target = target_ref[pick]
    place = lax.broadcasted_iota(jnp.int32, (rows_ref.shape[0], grad.shape[0]), 0)
    hit = jnp.logical_or(place == target[0:1, :], place == target[1:2, :])
    rows_ref[...] = jnp.dot(
        jnp.where(hit, 1.0, 0.0).astype(BF16), grad, preferred_element_type=F32
    ).astype(BF16)


def run_rows(pick, target_t, incoming, last_grad, slots):
    smem = pl.BlockSpec(memory_space=pltpu.SMEM)
    vmem = pl.BlockSpec(memory_space=pltpu.VMEM)
    return pl.pallas_call(
        rows_kernel,
        in_specs=[smem] + [vmem] * 3,
        out_specs=[vmem] * 2,
        out_shape=[
            jax.ShapeDtypeStruct(incoming.shape, BF16),
            jax.ShapeDtypeStruct((slots, incoming.shape[1]), BF16),
        ],
        name="rows",
    )(pick, target_t, incoming, last_grad)


def per_device(acts, out_grad, ln_gain, router, w_in, w_out, expert_ids, slot_ids, capacity):
    sections = lax.axis_size("section")
    section = lax.axis_index("section")
    me = lax.axis_index("expert")
    cores = lax.axis_size("dp")
    micro = acts.shape[1]
    tokens = acts.shape[2]
    width = acts.shape[3]
    experts = router.shape[2]
    top = expert_ids.shape[3]
    cap = 5 * tokens * top // (4 * experts)
    slots = experts * cap
    all_tokens = tokens * lax.axis_size("expert") * cores
    scale = 1.0 / math.sqrt(micro * all_tokens)
    tile = 512
    acts, ids, places, caps = acts[0], expert_ids[0], slot_ids[0], capacity[0]
    router_w = router[0]

    first_parts, second_parts = [w_in[0, 0]], [w_out[0, 0]]
    for by in range(1, cores):
        turn = [(i, (i + by) % cores) for i in range(cores)]
        first_parts.append(lax.ppermute(w_in[0, 0], "dp", turn))
    for by in range(1, cores):
        turn = [(i, (i + by) % cores) for i in range(cores)]
        second_parts.append(lax.ppermute(w_out[0, 0], "dp", turn))

    columns = jnp.arange(experts, dtype=jnp.int32)
    router_pad = jnp.zeros((LANES, width), BF16).at[:experts].set(router_w.T)
    pick_bool = ids[..., None] == columns
    table = pick_bool.astype(F32)
    kept = places < jnp.sum(jnp.where(pick_bool, caps[:, None, None, :], 0), axis=-1)
    target = jnp.where(kept, relative(ids, me, experts) * cap + places, -1)
    target_t = jnp.swapaxes(target, 1, 2)
    positions = jnp.arange(slots, dtype=jnp.int32)

    def forward_rows(m, grad):
        values = acts[m].astype(F32)
        centred = values - jnp.mean(values, axis=-1, keepdims=True)
        inverse = lax.rsqrt(jnp.mean(centred * centred, axis=-1, keepdims=True) + 1e-06)
        normed = (centred * inverse * ln_gain[0]).astype(BF16)
        logits = jnp.dot(normed, router_w, preferred_element_type=F32)
        chosen = jnp.sum(table[m] * logits[:, None, :], axis=2)
        gate1 = 1.0 / (1.0 + jnp.exp(chosen[:, 1] - chosen[:, 0]))
        gates = jnp.stack([gate1, 1.0 - gate1], axis=1)
        both = jnp.broadcast_to((gates[:, 0] * gates[:, 1])[:, None], gates.shape)
        meta = [table[m] - table[m][:, ::-1]]
        for values in split_hi_lo(gates) + split_hi_lo(both):
            meta.append(values[:, :, None].astype(F32))
        meta = jnp.concatenate(meta, axis=2)
        meta = jnp.pad(meta, ((0, 0), (0, 0), (0, LANES - meta.shape[2]))).astype(BF16)
        hit = (positions[:, None, None] == target[m][None]).astype(BF16)
        send = hit[:, :, 0] + hit[:, :, 1]
        sent = [jnp.dot(send, normed, preferred_element_type=F32).astype(BF16)]
        sent.append(
            jnp.einsum("ptk,tkc->pc", hit, meta, preferred_element_type=F32).astype(BF16)
        )
        if grad is not None:
            sent.append(jnp.dot(send, grad, preferred_element_type=F32).astype(BF16))
        return jnp.concatenate(sent, axis=1)

    def chunks_of(rows):
        return [rows[j * cap : (j + 1) * cap] for j in range(experts)]

    def picked(step):
        number = step - (sections - 1 - section)
        is_last = jnp.logical_and(section == sections - 1, step < micro)
        return jnp.stack([jnp.clip(number, 0, micro - 1), is_last.astype(jnp.int32)]).astype(jnp.int32)

    on_last = section == sections - 1
    grad0 = jnp.where(on_last, out_grad[0], jnp.zeros_like(out_grad[0]))
    packed0 = jnp.concatenate(exchange(chunks_of(forward_rows(0, grad0))), axis=0)
    split = width + LANES
    u0, grad_rows = packed0[None, :, :split], packed0[:, split:]
    rest = [forward_rows(m, None) for m in range(1, micro)]
    rest = exchange(
        [jnp.stack([rows[j * cap : (j + 1) * cap] for rows in rest]) for j in range(experts)]
    )
    stack = jnp.concatenate([u0, jnp.concatenate(rest, axis=1)], axis=0)

    sums = jnp.zeros((8 + -(-experts // 8) * 8, width), F32)
    gain = ln_gain
    grad = grad0
    steps = micro + sections - 1
    results = []
    down = [(i, i - 1) for i in range(1, sections)]
    for step in range(steps):
        pick = picked(step)
        rows_u = u0 if step == 0 else stack
        if step > 0:
            incoming = lax.ppermute(results[-1], "section", down)
            grad, sent = run_rows(pick, target_t, incoming, out_grad, slots)
            grad_rows = jnp.concatenate(exchange(chunks_of(sent)), axis=0)
        active, slope = run_hidden(pick, rows_u, first_parts, tile)
        slot_rows, sums = run_experts(
            pick, rows_u, grad_rows, active, slope, first_parts, second_parts,
            router_pad, gain, sums, experts, tile,
        )
        chunks = chunks_of(slot_rows)
        if step == steps - 1:
            tail = jnp.concatenate([sums[:1], sums[8 : 8 + experts]], axis=0).astype(BF16)
            tail = jnp.pad(tail, ((0, -(cap + 1 + experts) % 16), (0, 0)))
            chunks = [jnp.concatenate([chunk, tail], axis=0) for chunk in chunks]
        back = exchange(chunks, back=True)
        ret = jnp.concatenate([chunk[:cap] for chunk in back], axis=0)
        results.append(run_tokens(pick, acts, gain, target, ret, grad))

    total = sum(chunk[cap : cap + 1 + experts].astype(F32) for chunk in back)
    shared = total
    for by in range(1, cores):
        shared = shared + lax.ppermute(total, "dp", [(i, (i + by) % cores) for i in range(cores)])
    shared = shared * scale
    every = jnp.stack(results)
    grads = lax.dynamic_slice_in_dim(every, sections - 1 - section, micro, axis=0)
    return (grads[None], shared[:1], shared[1:].T[None])


def solution(mesh):
    return jax.shard_map(
        per_device,
        mesh=mesh,
        in_specs=(
            P("section", None, ("expert", "dp"), None),
            P(None, ("expert", "dp"), None),
            P("section", None),
            P("section", None, None),
            P("section", "expert", None, "dp"),
            P("section", "expert", "dp", None),
            P("section", None, ("expert", "dp"), None),
            P("section", None, ("expert", "dp"), None),
            P("section", None, None),
        ),
        out_specs=(
            P("section", None, ("expert", "dp"), None),
            P("section", None),
            P("section", None, None),
        ),
        check_vma=False,
    )
```

```python
import functools
import math

import jax
import jax.numpy as jnp
from jax import lax
from jax.experimental import pallas as pl
from jax.experimental.pallas import tpu as pltpu
from jax.sharding import PartitionSpec as P

GELU_C = math.sqrt(2.0 / math.pi)
LANES = 128
MIB = 1024 * 1024
F32 = jnp.float32
BF16 = jnp.bfloat16
NN = (((1,), (0,)), ((), ()))
NT = (((1,), (1,)), ((), ()))
TN = (((0,), (0,)), ((), ()))


def peers(count):
    if count & (count - 1) == 0:
        return [[(i, i ^ j) for i in range(count)] for j in range(1, count)]
    return [[(i, (i + j) % count) for i in range(count)] for j in range(1, count)]


def relative(ids, me, count):
    if count & (count - 1) == 0:
        return jnp.bitwise_xor(ids, me)
    away = ids - me
    return jnp.where(away < 0, away + count, away)


def picked(step, micro):
    sections = lax.axis_size("section")
    section = lax.axis_index("section")
    number = step - (sections - 1) + section
    return jnp.clip(number, 0, micro - 1), section == sections - 1


def exchange(chunks, back=False):
    count = len(chunks)
    out = [chunks[0]]
    for j, pairs in enumerate(peers(count), 1):
        moved = [(b, a) for a, b in pairs] if back else pairs
        out.append(lax.ppermute(chunks[j], "expert", moved))
    return out


def split_hi_lo(values):
    hi = values.astype(BF16)
    return hi, (values - hi.astype(F32)).astype(BF16)


def whole(kind, count):
    return [pl.BlockSpec(memory_space=kind)] * count


def prepare_kernel(
    acts_ref, gain_ref, router_ref, ids_ref, places_ref, caps_ref, *refs, micros, experts, cap, with_grad
):
    if with_grad:
        grad_ref, rows_ref, sel_ref, turned_ref = refs
    else:
        rows_ref, sel_ref, turned_ref = refs
    me = lax.axis_index("expert")
    tokens, width = acts_ref.shape[1:]
    slots = experts * cap
    lane = lax.broadcasted_iota(jnp.int32, (tokens, LANES), 1)
    place = lax.broadcasted_iota(jnp.int32, (slots, tokens), 0)
    across = lax.broadcasted_iota(jnp.int32, (tokens, slots), 1)
    square = [lax.broadcasted_iota(jnp.int32, (tokens, tokens), axis) for axis in (0, 1)]
    diagonal = square[0] == square[1]

    def column(row):
        spread = jnp.where(diagonal, jnp.broadcast_to(row.astype(F32), diagonal.shape), 0.0)
        return jnp.sum(spread, axis=1, keepdims=True).astype(jnp.int32)

    for at, m in enumerate(micros):
        values = acts_ref[m].astype(F32)
        centred = values - jnp.mean(values, axis=-1, keepdims=True)
        inverse = lax.rsqrt(jnp.mean(centred * centred, axis=-1, keepdims=True) + 1e-06)
        normed = (centred * inverse * gain_ref[...]).astype(BF16)
        logits = lax.dot_general(normed, router_ref[...], NT, preferred_element_type=F32)
        names = [ids_ref[m, k : k + 1, :] for k in range(2)]
        tables = [jnp.where(lane == column(name), 1.0, 0.0) for name in names]
        chosen = [jnp.sum(table * logits, axis=1, keepdims=True) for table in tables]
        gate1 = 1.0 / (1.0 + jnp.exp(chosen[1] - chosen[0]))
        gates = [gate1, 1.0 - gate1]
        both = gates[0] * gates[1]
        meta_rows = sel = turned = None
        for k in range(2):
            limit = jnp.zeros(names[k].shape, jnp.int32)
            for e in range(experts):
                limit = jnp.where(names[k] == e, caps_ref[m, e], limit)
            own = places_ref[m, k : k + 1, :]
            target = jnp.where(own < limit, relative(names[k], me, experts) * cap + own, -1)
            hit = jnp.where(place == target, 1.0, 0.0)
            hit_across = jnp.where(across == column(target), 1.0, 0.0)
            meta = tables[k] - tables[1 - k]
            for offset, value in enumerate(split_hi_lo(gates[k]) + split_hi_lo(both)):
                meta = jnp.where(lane == experts + offset, value.astype(F32), meta)
            part = jnp.dot(hit.astype(BF16), meta.astype(BF16), preferred_element_type=F32)
            meta_rows = part if k == 0 else meta_rows + part
            turned = hit if k == 0 else turned + hit
            sel = hit_across if k == 0 else sel + hit_across
        sel_ref[at] = sel.astype(BF16)
        turned = turned.astype(BF16)
        turned_ref[at] = turned
        rows = [jnp.dot(turned, normed, preferred_element_type=F32), meta_rows]
        if with_grad:
            grad = jnp.where(picked(0, 1)[1], grad_ref[m], jnp.zeros_like(grad_ref[m]))
            rows.append(jnp.dot(turned, grad, preferred_element_type=F32))
        begin = 0
        for piece in rows:
            end = begin + piece.shape[1]
            for j in range(experts):
                rows_ref[j, at, :, begin:end] = piece[j * cap : (j + 1) * cap].astype(BF16)
            begin = end


def run_prepare(acts, gain, router_pad, ids, places, caps, grad, micros, experts, cap):
    tokens, width = acts.shape[1:]
    slots, count = experts * cap, len(micros)
    packed = width + LANES + (0 if grad is None else width)
    args = [acts, gain, router_pad, ids, places]
    extra = [] if grad is None else [grad]
    return pl.pallas_call(
        functools.partial(
            prepare_kernel,
            micros=micros, experts=experts, cap=cap, with_grad=grad is not None,
        ),
        in_specs=whole(pltpu.VMEM, 5) + whole(pltpu.SMEM, 1) + whole(pltpu.VMEM, len(extra)),
        out_specs=whole(pltpu.VMEM, 3),
        out_shape=[
            jax.ShapeDtypeStruct((experts, count, cap, packed), BF16),
            jax.ShapeDtypeStruct((count, tokens, slots), BF16),
            jax.ShapeDtypeStruct((count, slots, tokens), BF16),
        ],
        compiler_params=pltpu.CompilerParams(vmem_limit_bytes=16 * MIB),
        name="prepare",
    )(*args, caps, *extra)


def turn_kernel(from_ref, to_ref, *, block):
    for at in range(0, from_ref.shape[0], block):
        to_ref[:, at : at + block] = from_ref[at : at + block, :].T


def run_turn(weights):
    rows, columns = weights.shape
    return pl.pallas_call(
        functools.partial(turn_kernel, block=256),
        in_specs=whole(pltpu.VMEM, 1),
        out_specs=pl.BlockSpec(memory_space=pltpu.VMEM),
        out_shape=jax.ShapeDtypeStruct((columns, rows), BF16),
        compiler_params=pltpu.CompilerParams(vmem_limit_bytes=8 * MIB),
        cost_estimate=pl.CostEstimate(
            flops=0, bytes_accessed=4 * rows * columns, transcendentals=0
        ),
        name="turn",
    )(weights)


def hidden_kernel(u_ref, *refs, step, width, tile):
    first_refs, (active_ref, slope_ref) = refs[:-2], refs[-2:]
    rows_u = u_ref[picked(step, u_ref.shape[0])[0], :, :width]
    at = 0
    for first_ref in first_refs:
        for begin in range(0, first_ref.shape[1], tile):
            hidden = jnp.dot(
                rows_u, first_ref[:, begin : begin + tile], preferred_element_type=F32
            )
            square = hidden * hidden
            tanh_val = jnp.tanh(hidden * (GELU_C + GELU_C * 0.044715 * square))
            up = 0.5 + 0.5 * tanh_val
            active_ref[:, at : at + tile] = (hidden * up).astype(BF16)
            rise = hidden * (GELU_C + GELU_C * 3.0 * 0.044715 * square)
            slope_ref[:, at : at + tile] = (up * (1.0 + (1.0 - tanh_val) * rise)).astype(BF16)
            at += tile


def run_hidden(step, stack, first_parts, tile):
    rows = stack.shape[1]
    width, part = first_parts[0].shape
    total = len(first_parts) * part
    out = jax.ShapeDtypeStruct((rows, total), BF16)
    return pl.pallas_call(
        functools.partial(hidden_kernel, step=step, width=width, tile=tile),
        in_specs=whole(pltpu.VMEM, 1 + len(first_parts)),
        out_specs=whole(pltpu.VMEM, 2),
        out_shape=[out, out],
        compiler_params=pltpu.CompilerParams(vmem_limit_bytes=20 * MIB),
        cost_estimate=pl.CostEstimate(
            flops=2 * rows * width * total,
            bytes_accessed=2 * width * total,
            transcendentals=rows * total,
        ),
        name="hidden",
    )(stack, *first_parts)


def expert_kernel(
    u_ref, grad_ref, active_ref, slope_ref, *refs, step, halves, width, experts, tile, first_way
):
    first_refs, second_refs = refs[:halves], refs[halves : 2 * halves]
    router_ref, gain_ref, *sums_in, out_ref, sums_ref, slot_acc = refs[2 * halves :]
    grads = grad_ref[...]
    gate_acc = None
    at = 0
    for first_ref, second_ref in zip(first_refs, second_refs):
        for begin in range(0, second_ref.shape[1], tile):
            back = jnp.dot(
                grads, second_ref[:, begin : begin + tile], preferred_element_type=F32
            )
            product = active_ref[:, at : at + tile].astype(F32) * back
            for lane in range(0, tile, LANES):
                piece = product[:, lane : lane + LANES]
                gate_acc = piece if gate_acc is None else gate_acc + piece
            pre = (back * slope_ref[:, at : at + tile].astype(F32)).astype(BF16)
            if first_way == NT:
                first = first_ref[:, begin : begin + tile]
            else:
                first = first_ref[begin : begin + tile, :]
            part = lax.dot_general(pre, first, first_way, preferred_element_type=F32)
            slot_acc[...] = part if at == 0 else slot_acc[...] + part
            at += tile

    pick, _ = picked(step, u_ref.shape[0])
    meta = u_ref[pick, :, width:].astype(F32)
    unit_gain = u_ref[pick, :, :width]
    gate = meta[:, experts : experts + 1] + meta[:, experts + 1 : experts + 2]
    both = meta[:, experts + 2 : experts + 3] + meta[:, experts + 3 : experts + 4]
    dots = jnp.sum(gate_acc, axis=1, keepdims=True)
    lane = lax.broadcasted_iota(jnp.int32, meta.shape, 1)
    dlogits = jnp.where(lane < experts, meta, 0.0) * (both * dots)
    high, low = split_hi_lo(dlogits)
    router_rows = jnp.dot(high, router_ref[...], preferred_element_type=F32) + jnp.dot(
        low, router_ref[...], preferred_element_type=F32
    )
    result = gate * slot_acc[...] + router_rows
    out_ref[...] = result.astype(BF16)
    gain_part = jnp.sum(result * unit_gain.astype(F32), axis=0, keepdims=True) / gain_ref[...]
    router_part = lax.dot_general(high, unit_gain, TN, preferred_element_type=F32)
    parts = [jnp.broadcast_to(gain_part, (8, width)), router_part[: sums_ref.shape[0] - 8, :]]
    for begin, part in zip((0, 8), parts):
        rows = slice(begin, begin + part.shape[0])
        sums_ref[rows, :] = sums_in[0][rows, :] + part if sums_in else part


def run_experts(
    step, stack, grad_rows, active, slope, first_parts, second_parts, router_pad, gain, sums,
    experts, tile, first_way,
):
    rows = stack.shape[1]
    width, part = second_parts[0].shape
    halves = len(first_parts)
    return pl.pallas_call(
        functools.partial(
            expert_kernel,
            step=step, halves=halves, width=width, experts=experts, tile=tile, first_way=first_way,
        ),
        in_specs=whole(pltpu.VMEM, 6 + len(sums) + 2 * halves),
        out_specs=whole(pltpu.VMEM, 2),
        out_shape=[
            jax.ShapeDtypeStruct((rows, width), BF16),
            jax.ShapeDtypeStruct((8 + -(-experts // 8) * 8, width), F32),
        ],
        scratch_shapes=[pltpu.VMEM((rows, width), F32)],
        compiler_params=pltpu.CompilerParams(vmem_limit_bytes=20 * MIB),
        cost_estimate=pl.CostEstimate(
            flops=4 * rows * width * halves * part,
            bytes_accessed=4 * width * halves * part,
            transcendentals=0,
        ),
        name="expert",
    )(
        stack, grad_rows, active, slope, *first_parts, *second_parts, router_pad, gain, *sums,
    )


def token_kernel(acts_ref, gain_ref, sel_ref, ret_ref, grad_ref, *refs, step):
    earlier, out_ref = refs[:-1], refs[-1]
    micro = acts_ref.shape[0]
    pick, is_last = picked(step, micro)
    values = acts_ref[pick].astype(F32)
    centred = values - jnp.mean(values, axis=-1, keepdims=True)
    inverse = lax.rsqrt(jnp.mean(centred * centred, axis=-1, keepdims=True) + 1e-06)
    unit = centred * inverse
    norm_grad = jnp.dot(sel_ref[pick], ret_ref[...], preferred_element_type=F32)
    scaled = norm_grad * gain_ref[...]
    change = inverse * (
        scaled
        - jnp.mean(scaled, axis=-1, keepdims=True)
        - unit * jnp.mean(scaled * unit, axis=-1, keepdims=True)
    )
    grad = grad_ref[...].astype(F32)
    if step == 0:
        grad = jnp.where(is_last, grad, jnp.zeros_like(grad))
    result = (grad + change).astype(BF16)
    if not earlier:
        out_ref[...] = result
        return
    sections = lax.axis_size("section")
    section = lax.axis_index("section")
    for at in range(sections):

        @pl.when(section == sections - 1 - at)
        def _(at=at):
            for m in range(micro):
                out_ref[m] = result if at + m == step else earlier[at + m][...]


def run_tokens(step, acts, gain, sel, ret, grad, earlier):
    shape = acts.shape if earlier else grad.shape
    return pl.pallas_call(
        functools.partial(token_kernel, step=step),
        in_specs=whole(pltpu.VMEM, 5 + len(earlier)),
        out_specs=pl.BlockSpec(memory_space=pltpu.VMEM),
        out_shape=jax.ShapeDtypeStruct(shape, BF16),
        compiler_params=pltpu.CompilerParams(vmem_limit_bytes=4 * MIB),
        name="token",
    )(acts, gain, sel, ret, grad, *earlier)


def rows_kernel(turned_ref, in_ref, *refs, step, cap):
    *last, grad_ref, rows_ref = refs
    pick, is_last = picked(step, turned_ref.shape[0])
    grad = in_ref[...]
    if last:
        grad = jnp.where(is_last, last[0][step], grad)
    grad_ref[...] = grad
    rows = jnp.dot(turned_ref[pick], grad, preferred_element_type=F32)
    for j in range(rows_ref.shape[0]):
        rows_ref[j] = rows[j * cap : (j + 1) * cap].astype(BF16)


def run_rows(step, turned, incoming, last_grad, experts, cap):
    last = [last_grad] if step < last_grad.shape[0] else []
    return pl.pallas_call(
        functools.partial(rows_kernel, step=step, cap=cap),
        in_specs=whole(pltpu.VMEM, 2 + len(last)),
        out_specs=whole(pltpu.VMEM, 2),
        out_shape=[
            jax.ShapeDtypeStruct(incoming.shape, BF16),
            jax.ShapeDtypeStruct((experts, cap, incoming.shape[1]), BF16),
        ],
        compiler_params=pltpu.CompilerParams(vmem_limit_bytes=4 * MIB),
        name="rows",
    )(turned, incoming, *last)


def per_device(acts, out_grad, ln_gain, router, w_in, w_out, expert_ids, slot_ids, capacity):
    sections = lax.axis_size("section")
    cores = lax.axis_size("dp")
    micro = acts.shape[1]
    tokens = acts.shape[2]
    width = acts.shape[3]
    experts = router.shape[2]
    top = expert_ids.shape[3]
    cap = 5 * tokens * top // (4 * experts)
    all_tokens = tokens * lax.axis_size("expert") * cores
    scale = 1.0 / math.sqrt(micro * all_tokens)
    tile = min(1024, w_in.shape[3])
    acts, caps, gain = acts[0], capacity[0], ln_gain
    ids, places = jnp.swapaxes(expert_ids[0], 1, 2), jnp.swapaxes(slot_ids[0], 1, 2)

    def both_halves(own):
        turns = [[(i, (i + by) % cores) for i in range(cores)] for by in range(1, cores)]
        return [own] + [lax.ppermute(own, "dp", pairs) for pairs in turns]

    first_parts = both_halves(w_in[0, 0])

    router_pad = jnp.pad(router[0].T, ((0, LANES - experts), (0, 0)))
    prepare = functools.partial(
        run_prepare, acts, gain, router_pad, ids, places, caps, experts=experts, cap=cap
    )

    sent, sel0, turned0 = prepare(grad=out_grad, micros=(0,))
    second_own, _ = lax.optimization_barrier((w_out[0, 0], sent))
    second_parts = both_halves(run_turn(second_own))
    packed0 = jnp.concatenate(exchange([sent[j, 0] for j in range(experts)]), axis=0)
    split = width + LANES
    u0, grad_rows = packed0[None, :, :split], packed0[:, split:]
    rest, sel, turned = prepare(grad=None, micros=tuple(range(1, micro)))
    sel = jnp.concatenate([sel0, sel], axis=0)
    turned = jnp.concatenate([turned0, turned], axis=0)

    sums = []
    grad = out_grad[0]
    steps = micro + sections - 1
    results = []
    down = [(i, i - 1) for i in range(1, sections)]
    for step in range(steps):
        if step == 0:
            rows_u = u0
        else:
            incoming = lax.ppermute(results[-1], "section", down)
            if step == 1:
                rest, _ = lax.optimization_barrier((rest, results[-1]))
                rest = exchange([rest[j] for j in range(experts)])
                rows_u = jnp.concatenate([u0, jnp.concatenate(rest, axis=1)], axis=0)
            grad, sent = run_rows(step, turned, incoming, out_grad, experts, cap)
            grad_rows = jnp.concatenate(exchange([sent[j] for j in range(experts)]), axis=0)
        active, slope = run_hidden(step, rows_u, first_parts, tile)
        slot_rows, shared = run_experts(
            step, rows_u, grad_rows, active, slope, first_parts if step == 0 else first_turned,
            second_parts, router_pad, gain, sums, experts, tile, NT if step == 0 else NN,
        )
        sums = [shared]
        if step == 0:
            first_own, _ = lax.optimization_barrier((w_in[0, 0], slot_rows))
            first_turned = both_halves(run_turn(first_own))
        chunks = [slot_rows[j * cap : (j + 1) * cap] for j in range(experts)]
        if step == steps - 1:
            tail = jnp.concatenate([shared[:1], shared[8 : 8 + experts]], axis=0).astype(BF16)
            tail = jnp.pad(tail, ((0, -(cap + 1 + experts) % 16), (0, 0)))
            chunks = [jnp.concatenate([chunk, tail], axis=0) for chunk in chunks]
        back = exchange(chunks, back=True)
        ret = jnp.concatenate([chunk[:cap] for chunk in back], axis=0)
        earlier = results if step == steps - 1 else []
        results.append(run_tokens(step, acts, gain, sel, ret, grad, earlier))

    total = sum(chunk[cap : cap + 1 + experts].astype(F32) for chunk in back)
    shared = total
    for by in range(1, cores):
        shared = shared + lax.ppermute(total, "dp", [(i, (i + by) % cores) for i in range(cores)])
    shared = shared * scale
    return (results[-1][None], shared[:1], shared[1:].T[None])


def solution(mesh):
    return jax.shard_map(
        per_device,
        mesh=mesh,
        in_specs=(
            P("section", None, ("expert", "dp"), None),
            P(None, ("expert", "dp"), None),
            P("section", None),
            P("section", None, None),
            P("section", "expert", None, "dp"),
            P("section", "expert", "dp", None),
            P("section", None, ("expert", "dp"), None),
            P("section", None, ("expert", "dp"), None),
            P("section", None, None),
        ),
        out_specs=(
            P("section", None, ("expert", "dp"), None),
            P("section", None),
            P("section", None, None),
        ),
        check_vma=False,
    )
```

```python
import functools
import math

import jax
import jax.numpy as jnp
from jax import lax
from jax.experimental import pallas as pl
from jax.experimental.pallas import tpu as pltpu
from jax.sharding import PartitionSpec as P

GELU_C = math.sqrt(2.0 / math.pi)
LANES = 128
HALF = LANES // 2
MIB = 1024 * 1024
F32 = jnp.float32
BF16 = jnp.bfloat16
NN = (((1,), (0,)), ((), ()))
NT = (((1,), (1,)), ((), ()))
TN = (((0,), (0,)), ((), ()))


def peers(count):
    if count & (count - 1) == 0:
        return [[(i, i ^ j) for i in range(count)] for j in range(1, count)]
    return [[(i, (i + j) % count) for i in range(count)] for j in range(1, count)]


def relative(ids, me, count):
    if count & (count - 1) == 0:
        return jnp.bitwise_xor(ids, me)
    away = ids - me
    return jnp.where(away < 0, away + count, away)


def picked(step, micro):
    sections = lax.axis_size("section")
    section = lax.axis_index("section")
    number = step - (sections - 1) + section
    return jnp.clip(number, 0, micro - 1), section == sections - 1


def exchange(chunks, back=False):
    count = len(chunks)
    out = [chunks[0]]
    for j, pairs in enumerate(peers(count), 1):
        moved = [(b, a) for a, b in pairs] if back else pairs
        out.append(lax.ppermute(chunks[j], "expert", moved))
    return out


def split_hi_lo(values):
    hi = values.astype(BF16)
    return hi, (values - hi.astype(F32)).astype(BF16)


def whole(kind, count):
    return [pl.BlockSpec(memory_space=kind)] * count


def prepare_kernel(*refs, micros, experts, cap, with_grad):
    count = 6 + with_grad
    rows_ref, sel_ref, turned_ref, router_ref, kept_ref = refs[count + 1 : count + 6]
    *held, sems = refs[count + 6 :]
    keep = pltpu.make_async_copy(refs[count], kept_ref, sems.at[count])
    sources = [refs[0].at[pl.ds(micros[0], len(micros))]] + list(refs[1:6])
    if with_grad:
        sources.append(refs[6].at[pl.ds(micros[0], len(micros))])
    copies = [
        pltpu.make_async_copy(source, to, sems.at[i])
        for i, (source, to) in enumerate(zip(sources, held))
    ]
    for copy in copies + [keep]:
        copy.start()
    acts_ref, gain_ref, own_router_ref, ids_ref, places_ref, caps_ref = held[:6]
    me = lax.axis_index("expert")
    tokens, width = acts_ref.shape[1:]
    slots = experts * cap
    lane = lax.broadcasted_iota(jnp.int32, (tokens, LANES), 1)
    place = lax.broadcasted_iota(jnp.int32, (slots, tokens), 0)
    across = lax.broadcasted_iota(jnp.int32, (tokens, slots), 1)
    square = [lax.broadcasted_iota(jnp.int32, (tokens, tokens), axis) for axis in (0, 1)]
    diagonal = square[0] == square[1]

    def column(row):
        spread = jnp.where(diagonal, jnp.broadcast_to(row.astype(F32), diagonal.shape), 0.0)
        return jnp.sum(spread, axis=1, keepdims=True).astype(jnp.int32)

    for copy in copies:
        copy.wait()
    name = lax.broadcasted_iota(jnp.int32, (LANES, experts), 0) % HALF
    twice = jnp.where(name == lax.broadcasted_iota(jnp.int32, name.shape, 1), 1.0, 0.0)
    router_ref[...] = jnp.dot(
        twice.astype(BF16), own_router_ref[...], preferred_element_type=F32
    ).astype(BF16)
    for at, m in enumerate(micros):
        values = acts_ref[at].astype(F32)
        centred = values - jnp.mean(values, axis=-1, keepdims=True)
        inverse = lax.rsqrt(jnp.mean(centred * centred, axis=-1, keepdims=True) + 1e-06)
        normed = (centred * inverse * gain_ref[...]).astype(BF16)
        logits = lax.dot_general(normed, router_ref[...], NT, preferred_element_type=F32)
        names = [ids_ref[m, k : k + 1, :] for k in range(2)]
        tables = [jnp.where(lane % HALF == column(name), 1.0, 0.0) for name in names]
        chosen = [0.5 * jnp.sum(table * logits, axis=1, keepdims=True) for table in tables]
        gate1 = 1.0 / (1.0 + jnp.exp(chosen[1] - chosen[0]))
        gates = [gate1, 1.0 - gate1]
        both = gates[0] * gates[1]
        pairs = [tables[0] - tables[1], tables[1] - tables[0]]
        meta_rows = sel = turned = None
        for k in range(2):
            limit = jnp.zeros(names[k].shape, jnp.int32)
            for e in range(experts):
                limit = jnp.where(names[k] == e, caps_ref[m, :, e : e + 1], limit)
            own = places_ref[m, k : k + 1, :]
            target = jnp.where(own < limit, relative(names[k], me, experts) * cap + own, -1)
            hit = jnp.where(place == target, 1.0, 0.0)
            hit_across = jnp.where(across == column(target), 1.0, 0.0)
            meta = pairs[k]
            for offset, value in enumerate(split_hi_lo(gates[k]) + split_hi_lo(both)):
                meta = jnp.where(lane == experts + offset, value.astype(F32), meta)
            part = jnp.dot(hit.astype(BF16), meta.astype(BF16), preferred_element_type=F32)
            meta_rows = part if k == 0 else meta_rows + part
            turned = hit if k == 0 else turned + hit
            sel = hit_across if k == 0 else sel + hit_across
        sel_ref[at] = sel.astype(BF16)
        turned = turned.astype(BF16)
        turned_ref[at] = turned
        rows = [jnp.dot(turned, normed, preferred_element_type=F32), meta_rows]
        if with_grad:
            grad = held[6][at]
            grad = jnp.where(picked(0, 1)[1], grad, jnp.zeros_like(grad))
            rows.append(jnp.dot(turned, grad, preferred_element_type=F32))
        begin = 0
        for piece in rows:
            end = begin + piece.shape[1]
            for j in range(experts):
                rows_ref[j, at, :, begin:end] = piece[j * cap : (j + 1) * cap].astype(BF16)
            begin = end
    keep.wait()


def run_prepare(inputs, grad, weights, micros, cap):
    _, tokens, width = inputs[0].shape
    experts = inputs[2].shape[0]
    slots, count = experts * cap, len(micros)
    packed = width + LANES + (0 if grad is None else width)
    copied = list(inputs) + ([] if grad is None else [grad])
    taken = [pltpu.with_memory_space_constraint(array, pltpu.HBM) for array in copied + [weights]]
    scratch = [pltpu.VMEM(array.shape, array.dtype) for array in copied]
    for at in (0, 6)[: 1 + (grad is not None)]:
        scratch[at] = pltpu.VMEM((count, tokens, width), BF16)
    return pl.pallas_call(
        functools.partial(
            prepare_kernel,
            micros=micros, experts=experts, cap=cap, with_grad=grad is not None,
        ),
        in_specs=whole(pltpu.HBM, len(taken)),
        out_specs=whole(pltpu.VMEM, 5),
        out_shape=[
            jax.ShapeDtypeStruct((experts, count, cap, packed), BF16),
            jax.ShapeDtypeStruct((count, tokens, slots), BF16),
            jax.ShapeDtypeStruct((count, slots, tokens), BF16),
            jax.ShapeDtypeStruct((LANES, width), BF16),
            jax.ShapeDtypeStruct(weights.shape, BF16),
        ],
        scratch_shapes=scratch + [pltpu.SemaphoreType.DMA((len(taken),))],
        compiler_params=pltpu.CompilerParams(vmem_limit_bytes=16 * MIB),
        name="prepare",
    )(*taken)


def turn_kernel(from_ref, to_ref, *, block):
    for at in range(0, from_ref.shape[0], block):
        to_ref[:, at : at + block] = from_ref[at : at + block, :].T


def run_turn(weights):
    rows, columns = weights.shape
    return pl.pallas_call(
        functools.partial(turn_kernel, block=256),
        in_specs=whole(pltpu.VMEM, 1),
        out_specs=pl.BlockSpec(memory_space=pltpu.VMEM),
        out_shape=jax.ShapeDtypeStruct((columns, rows), BF16),
        compiler_params=pltpu.CompilerParams(vmem_limit_bytes=8 * MIB),
        cost_estimate=pl.CostEstimate(
            flops=0, bytes_accessed=4 * rows * columns, transcendentals=0
        ),
        name="turn",
    )(weights)


def hidden_kernel(u_ref, *refs, step, width, tile):
    first_refs, (active_ref, slope_ref) = refs[:-2], refs[-2:]
    rows_u = u_ref[picked(step, u_ref.shape[0])[0], :, :width]
    at = 0
    for first_ref in first_refs:
        for begin in range(0, first_ref.shape[1], tile):
            hidden = jnp.dot(
                rows_u, first_ref[:, begin : begin + tile], preferred_element_type=F32
            )
            square = hidden * hidden
            tanh_val = jnp.tanh(hidden * (GELU_C + GELU_C * 0.044715 * square))
            up = 0.5 + 0.5 * tanh_val
            active_ref[:, at : at + tile] = (hidden * up).astype(BF16)
            rise = hidden * (GELU_C + GELU_C * 3.0 * 0.044715 * square)
            slope_ref[:, at : at + tile] = (up * (1.0 + (1.0 - tanh_val) * rise)).astype(BF16)
            at += tile


def run_hidden(step, stack, first_parts, tile):
    rows = stack.shape[1]
    width, part = first_parts[0].shape
    total = len(first_parts) * part
    out = jax.ShapeDtypeStruct((rows, total), BF16)
    return pl.pallas_call(
        functools.partial(hidden_kernel, step=step, width=width, tile=tile),
        in_specs=whole(pltpu.VMEM, 1 + len(first_parts)),
        out_specs=whole(pltpu.VMEM, 2),
        out_shape=[out, out],
        compiler_params=pltpu.CompilerParams(vmem_limit_bytes=20 * MIB),
        cost_estimate=pl.CostEstimate(
            flops=2 * rows * width * total,
            bytes_accessed=2 * width * total,
            transcendentals=rows * total,
        ),
        name="hidden",
    )(stack, *first_parts)


def expert_kernel(
    u_ref, grad_ref, active_ref, slope_ref, *refs, step, halves, width, experts, tile, way
):
    first_refs, second_refs = refs[:halves], refs[halves : 2 * halves]
    router_ref, gain_ref, *sums_in, out_ref, sums_ref, slot_acc = refs[2 * halves :]
    grads = grad_ref[...]
    gate_acc = None
    at = 0
    def hidden_part(ref, axis, begin):
        return ref[begin : begin + tile, :] if axis == 0 else ref[:, begin : begin + tile]

    straight = way == NN
    for first_ref, second_ref in zip(first_refs, second_refs):
        for begin in range(0, second_ref.shape[1 if straight else 0], tile):
            second = hidden_part(second_ref, 1 if straight else 0, begin)
            back = lax.dot_general(grads, second, way, preferred_element_type=F32)
            product = active_ref[:, at : at + tile].astype(F32) * back
            for lane in range(0, tile, LANES):
                piece = product[:, lane : lane + LANES]
                gate_acc = piece if gate_acc is None else gate_acc + piece
            pre = (back * slope_ref[:, at : at + tile].astype(F32)).astype(BF16)
            first = hidden_part(first_ref, 0 if straight else 1, begin)
            part = lax.dot_general(pre, first, way, preferred_element_type=F32)
            slot_acc[...] = part if at == 0 else slot_acc[...] + part
            at += tile

    pick, _ = picked(step, u_ref.shape[0])
    meta = u_ref[pick, :, width:].astype(F32)
    unit_gain = u_ref[pick, :, :width]
    gate = meta[:, experts : experts + 1] + meta[:, experts + 1 : experts + 2]
    both = meta[:, experts + 2 : experts + 3] + meta[:, experts + 3 : experts + 4]
    dots = jnp.sum(gate_acc, axis=1, keepdims=True)
    lane = lax.broadcasted_iota(jnp.int32, meta.shape, 1)
    dlogits = jnp.where(lane % HALF < experts, meta, 0.0) * (both * dots)
    high, low = split_hi_lo(dlogits)
    parts = jnp.where(lane < HALF, high, low)
    router_rows = jnp.dot(parts, router_ref[...], preferred_element_type=F32)
    result = gate * slot_acc[...] + router_rows
    out_ref[...] = result.astype(BF16)
    gain_part = jnp.sum(result * unit_gain.astype(F32), axis=0, keepdims=True) / gain_ref[...]
    router_part = lax.dot_general(parts, unit_gain, TN, preferred_element_type=F32)
    parts = [jnp.broadcast_to(gain_part, (8, width)), router_part[: sums_ref.shape[0] - 8, :]]
    for begin, part in zip((0, 8), parts):
        rows = slice(begin, begin + part.shape[0])
        sums_ref[rows, :] = sums_in[0][rows, :] + part if sums_in else part


def run_experts(
    step, stack, grad_rows, active, slope, first_parts, second_parts, router_pad, gain, sums,
    experts, tile, way,
):
    rows = stack.shape[1]
    width, part = grad_rows.shape[1], first_parts[0].size // grad_rows.shape[1]
    halves = len(first_parts)
    return pl.pallas_call(
        functools.partial(
            expert_kernel,
            step=step, halves=halves, width=width, experts=experts, tile=tile, way=way,
        ),
        in_specs=whole(pltpu.VMEM, 6 + len(sums) + 2 * halves),
        out_specs=whole(pltpu.VMEM, 2),
        out_shape=[
            jax.ShapeDtypeStruct((rows, width), BF16),
            jax.ShapeDtypeStruct((8 + -(-experts // 8) * 8, width), F32),
        ],
        scratch_shapes=[pltpu.VMEM((rows, width), F32)],
        compiler_params=pltpu.CompilerParams(vmem_limit_bytes=20 * MIB),
        cost_estimate=pl.CostEstimate(
            flops=4 * rows * width * halves * part,
            bytes_accessed=4 * width * halves * part,
            transcendentals=0,
        ),
        name="expert",
    )(
        stack, grad_rows, active, slope, *first_parts, *second_parts, router_pad, gain, *sums,
    )


def token_kernel(acts_ref, gain_ref, sel_ref, ret_ref, grad_ref, *refs, step):
    earlier, out_ref = refs[:-1], refs[-1]
    micro = acts_ref.shape[0]
    pick, is_last = picked(step, micro)
    values = acts_ref[pick].astype(F32)
    centred = values - jnp.mean(values, axis=-1, keepdims=True)
    inverse = lax.rsqrt(jnp.mean(centred * centred, axis=-1, keepdims=True) + 1e-06)
    unit = centred * inverse
    norm_grad = jnp.dot(sel_ref[pick], ret_ref[...], preferred_element_type=F32)
    scaled = norm_grad * gain_ref[...]
    change = inverse * (
        scaled
        - jnp.mean(scaled, axis=-1, keepdims=True)
        - unit * jnp.mean(scaled * unit, axis=-1, keepdims=True)
    )
    grad = grad_ref[...].astype(F32)
    if step == 0:
        grad = jnp.where(is_last, grad, jnp.zeros_like(grad))
    result = (grad + change).astype(BF16)
    if not earlier:
        out_ref[...] = result
        return
    sections = lax.axis_size("section")
    section = lax.axis_index("section")
    for at in range(sections):

        @pl.when(section == sections - 1 - at)
        def _(at=at):
            for m in range(micro):
                out_ref[m] = result if at + m == step else earlier[at + m][...]


def run_tokens(step, acts, gain, sel, ret, grad, earlier):
    shape = acts.shape if earlier else grad.shape
    return pl.pallas_call(
        functools.partial(token_kernel, step=step),
        in_specs=whole(pltpu.VMEM, 5 + len(earlier)),
        out_specs=pl.BlockSpec(memory_space=pltpu.VMEM),
        out_shape=jax.ShapeDtypeStruct(shape, BF16),
        compiler_params=pltpu.CompilerParams(vmem_limit_bytes=4 * MIB),
        name="token",
    )(acts, gain, sel, ret, grad, *earlier)


def rows_kernel(turned_ref, in_ref, *refs, step, cap):
    *last, grad_ref, rows_ref = refs
    pick, is_last = picked(step, turned_ref.shape[0])
    grad = in_ref[...]
    if last:
        grad = jnp.where(is_last, last[0][step], grad)
    grad_ref[...] = grad
    rows = jnp.dot(turned_ref[pick], grad, preferred_element_type=F32)
    for j in range(rows_ref.shape[0]):
        rows_ref[j] = rows[j * cap : (j + 1) * cap].astype(BF16)


def run_rows(step, turned, incoming, last_grad, experts, cap):
    last = [last_grad] if step < last_grad.shape[0] else []
    return pl.pallas_call(
        functools.partial(rows_kernel, step=step, cap=cap),
        in_specs=whole(pltpu.VMEM, 2 + len(last)),
        out_specs=whole(pltpu.VMEM, 2),
        out_shape=[
            jax.ShapeDtypeStruct(incoming.shape, BF16),
            jax.ShapeDtypeStruct((experts, cap, incoming.shape[1]), BF16),
        ],
        compiler_params=pltpu.CompilerParams(vmem_limit_bytes=4 * MIB),
        name="rows",
    )(turned, incoming, *last)


def per_device(acts, out_grad, ln_gain, router, w_in, w_out, expert_ids, slot_ids, capacity):
    sections = lax.axis_size("section")
    cores = lax.axis_size("dp")
    micro = acts.shape[1]
    tokens = acts.shape[2]
    width = acts.shape[3]
    experts = router.shape[2]
    top = expert_ids.shape[3]
    cap = 5 * tokens * top // (4 * experts)
    all_tokens = tokens * lax.axis_size("expert") * cores
    scale = 1.0 / math.sqrt(micro * all_tokens)
    tile = min(1024, w_in.shape[3])
    acts, caps, gain = acts[0], capacity[0], ln_gain
    ids, places = jnp.swapaxes(expert_ids[0], 1, 2), jnp.swapaxes(slot_ids[0], 1, 2)
    inputs = (acts, gain, router[0].T, ids, places, caps[:, None, :])

    def both_halves(own):
        turns = [[(i, (i + by) % cores) for i in range(cores)] for by in range(1, cores)]
        return [own] + [lax.ppermute(own, "dp", pairs) for pairs in turns]

    first_parts = both_halves(w_in[0, 0])
    second_parts = both_halves(w_out[0, 0])

    sent, sel0, turned0, router_pad, first_own = run_prepare(inputs, out_grad, w_in[0, 0], (0,), cap)
    first_parts[0] = first_own
    packed0 = jnp.concatenate(exchange([sent[j, 0] for j in range(experts)]), axis=0)
    split = width + LANES
    u0, grad_rows = packed0[None, :, :split], packed0[:, split:]
    rest, sel, turned, _, second_own = run_prepare(
        inputs, None, w_out[0, 0], tuple(range(1, micro)), cap
    )
    second_parts[0] = second_own
    own_turned = [run_turn(part) for part in (first_own, second_own)]
    rest = exchange([rest[j] for j in range(experts)])
    stack = jnp.concatenate([u0, jnp.concatenate(rest, axis=1)], axis=0)
    sel = jnp.concatenate([sel0, sel], axis=0)
    turned = jnp.concatenate([turned0, turned], axis=0)

    rows_u = u0
    sums = []
    grad = out_grad[0]
    steps = micro + sections - 1
    results = []
    down = [(i, i - 1) for i in range(1, sections)]
    for step in range(steps):
        if step > 0:
            rows_u = stack
            incoming = lax.ppermute(results[-1], "section", down)
            grad, sent = run_rows(step, turned, incoming, out_grad, experts, cap)
            grad_rows = jnp.concatenate(exchange([sent[j] for j in range(experts)]), axis=0)
        active, slope = run_hidden(step, rows_u, first_parts, tile)
        slot_rows, shared = run_experts(
            step, rows_u, grad_rows, active, slope, first_parts if step == 0 else first_turned,
            second_parts if step == 0 else second_turned, router_pad, gain, sums, experts, tile,
            NT if step == 0 else NN,
        )
        sums = [shared]
        if step == 0:
            others = first_parts[1:] + second_parts[1:]
            others, _ = lax.optimization_barrier((others, slot_rows))
            others = [run_turn(part) for part in others]
            first_turned = own_turned[:1] + others[: cores - 1]
            second_turned = own_turned[1:] + others[cores - 1 :]
        chunks = [slot_rows[j * cap : (j + 1) * cap] for j in range(experts)]
        if step == steps - 1:
            tail = jnp.concatenate([shared[:1], shared[8 : 8 + experts]], axis=0).astype(BF16)
            tail = jnp.pad(tail, ((0, -(cap + 1 + experts) % 16), (0, 0)))
            chunks = [jnp.concatenate([chunk, tail], axis=0) for chunk in chunks]
        back = exchange(chunks, back=True)
        ret = jnp.concatenate([chunk[:cap] for chunk in back], axis=0)
        earlier = results if step == steps - 1 else []
        results.append(run_tokens(step, acts, gain, sel, ret, grad, earlier))

    total = sum(chunk[cap : cap + 1 + experts].astype(F32) for chunk in back)
    shared = total
    for by in range(1, cores):
        shared = shared + lax.ppermute(total, "dp", [(i, (i + by) % cores) for i in range(cores)])
    shared = shared * scale
    return (results[-1][None], shared[:1], shared[1:].T[None])


def solution(mesh):
    return jax.shard_map(
        per_device,
        mesh=mesh,
        in_specs=(
            P("section", None, ("expert", "dp"), None),
            P(None, ("expert", "dp"), None),
            P("section", None),
            P("section", None, None),
            P("section", "expert", None, "dp"),
            P("section", "expert", "dp", None),
            P("section", None, ("expert", "dp"), None),
            P("section", None, ("expert", "dp"), None),
            P("section", None, None),
        ),
        out_specs=(
            P("section", None, ("expert", "dp"), None),
            P("section", None),
            P("section", None, None),
        ),
        check_vma=False,
    )
```

```python
import functools
import math

import jax
import jax.numpy as jnp
from jax import lax
from jax.experimental import pallas as pl
from jax.experimental.pallas import tpu as pltpu
from jax.sharding import PartitionSpec as P

GELU_C = math.sqrt(2.0 / math.pi)
LANES = 128
HALF = LANES // 2
MIB = 1024 * 1024
F32 = jnp.float32
BF16 = jnp.bfloat16
NN = (((1,), (0,)), ((), ()))
NT = (((1,), (1,)), ((), ()))
TN = (((0,), (0,)), ((), ()))


def peers(count):
    if count & (count - 1) == 0:
        return [[(i, i ^ j) for i in range(count)] for j in range(1, count)]
    return [[(i, (i + j) % count) for i in range(count)] for j in range(1, count)]


def relative(ids, me, count):
    if count & (count - 1) == 0:
        return jnp.bitwise_xor(ids, me)
    away = ids - me
    return jnp.where(away < 0, away + count, away)


def picked(step, micro):
    sections = lax.axis_size("section")
    section = lax.axis_index("section")
    number = step - (sections - 1) + section
    return jnp.clip(number, 0, micro - 1), section == sections - 1, number


def exchange(chunks, back=False):
    count = len(chunks)
    out = [chunks[0]]
    for j, pairs in enumerate(peers(count), 1):
        moved = [(b, a) for a, b in pairs] if back else pairs
        out.append(lax.ppermute(chunks[j], "expert", moved))
    return out


def split_hi_lo(values):
    hi = values.astype(BF16)
    return hi, (values - hi.astype(F32)).astype(BF16)


def whole(kind, count):
    return [pl.BlockSpec(memory_space=kind)] * count


def prepare_kernel(*refs, micros, experts, cap, with_grad):
    count = 6 + with_grad
    rows_ref, sel_ref, turned_ref, router_ref, kept_ref = refs[count + 1 : count + 6]
    *held, sems = refs[count + 6 :]
    keep = pltpu.make_async_copy(refs[count], kept_ref, sems.at[count])
    sources = [refs[0].at[pl.ds(micros[0], len(micros))]] + list(refs[1:6])
    if with_grad:
        sources.append(refs[6].at[pl.ds(micros[0], len(micros))])
    copies = [
        pltpu.make_async_copy(source, to, sems.at[i])
        for i, (source, to) in enumerate(zip(sources, held))
    ]
    for copy in copies + [keep]:
        copy.start()
    acts_ref, gain_ref, own_router_ref, ids_ref, places_ref, caps_ref = held[:6]
    me = lax.axis_index("expert")
    tokens, width = acts_ref.shape[1:]
    slots = experts * cap
    lane = lax.broadcasted_iota(jnp.int32, (tokens, LANES), 1)
    place = lax.broadcasted_iota(jnp.int32, (slots, tokens), 0)
    across = lax.broadcasted_iota(jnp.int32, (tokens, slots), 1)
    square = [lax.broadcasted_iota(jnp.int32, (tokens, tokens), axis) for axis in (0, 1)]
    diagonal = square[0] == square[1]

    def column(row):
        spread = jnp.where(diagonal, jnp.broadcast_to(row.astype(F32), diagonal.shape), 0.0)
        return jnp.sum(spread, axis=1, keepdims=True).astype(jnp.int32)

    for copy in copies:
        copy.wait()
    name = lax.broadcasted_iota(jnp.int32, (LANES, experts), 0) % HALF
    twice = jnp.where(name == lax.broadcasted_iota(jnp.int32, name.shape, 1), 1.0, 0.0)
    router_ref[...] = jnp.dot(
        twice.astype(BF16), own_router_ref[...], preferred_element_type=F32
    ).astype(BF16)
    for at, m in enumerate(micros):
        values = acts_ref[at].astype(F32)
        centred = values - jnp.mean(values, axis=-1, keepdims=True)
        inverse = lax.rsqrt(jnp.mean(centred * centred, axis=-1, keepdims=True) + 1e-06)
        normed = (centred * inverse * gain_ref[...]).astype(BF16)
        logits = lax.dot_general(normed, router_ref[...], NT, preferred_element_type=F32)
        names = [ids_ref[m, k : k + 1, :] for k in range(2)]
        tables = [jnp.where(lane % HALF == column(name), 1.0, 0.0) for name in names]
        chosen = [0.5 * jnp.sum(table * logits, axis=1, keepdims=True) for table in tables]
        gate1 = 1.0 / (1.0 + jnp.exp(chosen[1] - chosen[0]))
        gates = [gate1, 1.0 - gate1]
        both = gates[0] * gates[1]
        pairs = [tables[0] - tables[1], tables[1] - tables[0]]
        meta_rows = sel = turned = None
        for k in range(2):
            limit = jnp.zeros(names[k].shape, jnp.int32)
            for e in range(experts):
                limit = jnp.where(names[k] == e, caps_ref[m, :, e : e + 1], limit)
            own = places_ref[m, k : k + 1, :]
            target = jnp.where(own < limit, relative(names[k], me, experts) * cap + own, -1)
            hit = jnp.where(place == target, 1.0, 0.0)
            hit_across = jnp.where(across == column(target), 1.0, 0.0)
            meta = pairs[k]
            for offset, value in enumerate(split_hi_lo(gates[k]) + split_hi_lo(both)):
                meta = jnp.where(lane == experts + offset, value.astype(F32), meta)
            part = jnp.dot(hit.astype(BF16), meta.astype(BF16), preferred_element_type=F32)
            meta_rows = part if k == 0 else meta_rows + part
            turned = hit if k == 0 else turned + hit
            sel = hit_across if k == 0 else sel + hit_across
        sel_ref[at] = sel.astype(BF16)
        turned = turned.astype(BF16)
        turned_ref[at] = turned
        rows = [jnp.dot(turned, normed, preferred_element_type=F32), meta_rows]
        if with_grad:
            grad = held[6][at]
            grad = jnp.where(picked(0, 1)[1], grad, jnp.zeros_like(grad))
            rows.append(jnp.dot(turned, grad, preferred_element_type=F32))
        begin = 0
        for piece in rows:
            end = begin + piece.shape[1]
            for j in range(experts):
                rows_ref[j, at, :, begin:end] = piece[j * cap : (j + 1) * cap].astype(BF16)
            begin = end
    keep.wait()


def run_prepare(inputs, grad, weights, micros, cap):
    _, tokens, width = inputs[0].shape
    experts = inputs[2].shape[0]
    slots, count = experts * cap, len(micros)
    packed = width + LANES + (0 if grad is None else width)
    copied = list(inputs) + ([] if grad is None else [grad])
    taken = [pltpu.with_memory_space_constraint(array, pltpu.HBM) for array in copied + [weights]]
    scratch = [pltpu.VMEM(array.shape, array.dtype) for array in copied]
    for at in (0, 6)[: 1 + (grad is not None)]:
        scratch[at] = pltpu.VMEM((count, tokens, width), BF16)
    return pl.pallas_call(
        functools.partial(
            prepare_kernel,
            micros=micros, experts=experts, cap=cap, with_grad=grad is not None,
        ),
        in_specs=whole(pltpu.HBM, len(taken)),
        out_specs=whole(pltpu.VMEM, 5),
        out_shape=[
            jax.ShapeDtypeStruct((experts, count, cap, packed), BF16),
            jax.ShapeDtypeStruct((count, tokens, slots), BF16),
            jax.ShapeDtypeStruct((count, slots, tokens), BF16),
            jax.ShapeDtypeStruct((LANES, width), BF16),
            jax.ShapeDtypeStruct(weights.shape, BF16),
        ],
        scratch_shapes=scratch + [pltpu.SemaphoreType.DMA((len(taken),))],
        compiler_params=pltpu.CompilerParams(vmem_limit_bytes=16 * MIB),
        name="prepare",
    )(*taken)


def turn_kernel(from_ref, to_ref, *, block):
    for at in range(0, from_ref.shape[0], block):
        to_ref[:, at : at + block] = from_ref[at : at + block, :].T


def run_turn(weights):
    rows, columns = weights.shape
    return pl.pallas_call(
        functools.partial(turn_kernel, block=256),
        in_specs=whole(pltpu.VMEM, 1),
        out_specs=pl.BlockSpec(memory_space=pltpu.VMEM),
        out_shape=jax.ShapeDtypeStruct((columns, rows), BF16),
        compiler_params=pltpu.CompilerParams(vmem_limit_bytes=8 * MIB),
        cost_estimate=pl.CostEstimate(
            flops=0, bytes_accessed=4 * rows * columns, transcendentals=0
        ),
        name="turn",
    )(weights)


def hidden_kernel(u_ref, *refs, step, width, tile):
    first_refs, (active_ref, slope_ref) = refs[:-2], refs[-2:]
    rows_u = u_ref[picked(step, u_ref.shape[0])[0], :, :width]
    at = 0
    for first_ref in first_refs:
        for begin in range(0, first_ref.shape[1], tile):
            hidden = jnp.dot(
                rows_u, first_ref[:, begin : begin + tile], preferred_element_type=F32
            )
            square = hidden * hidden
            tanh_val = jnp.tanh(hidden * (GELU_C + GELU_C * 0.044715 * square))
            up = 0.5 + 0.5 * tanh_val
            active_ref[:, at : at + tile] = (hidden * up).astype(BF16)
            rise = hidden * (GELU_C + GELU_C * 3.0 * 0.044715 * square)
            slope_ref[:, at : at + tile] = (up * (1.0 + (1.0 - tanh_val) * rise)).astype(BF16)
            at += tile


def run_hidden(step, stack, first_parts, tile):
    rows = stack.shape[1]
    width, part = first_parts[0].shape
    total = len(first_parts) * part
    out = jax.ShapeDtypeStruct((rows, total), BF16)
    return pl.pallas_call(
        functools.partial(hidden_kernel, step=step, width=width, tile=tile),
        in_specs=whole(pltpu.VMEM, 1 + len(first_parts)),
        out_specs=whole(pltpu.VMEM, 2),
        out_shape=[out, out],
        compiler_params=pltpu.CompilerParams(vmem_limit_bytes=20 * MIB),
        cost_estimate=pl.CostEstimate(
            flops=2 * rows * width * total,
            bytes_accessed=2 * width * total,
            transcendentals=rows * total,
        ),
        name="hidden",
    )(stack, *first_parts)


def expert_kernel(
    u_ref, grad_ref, active_ref, slope_ref, *refs, step, halves, width, experts, tile, ways
):
    first_refs, second_refs = refs[:halves], refs[halves : 2 * halves]
    router_ref, gain_ref, *sums_in, out_ref, sums_ref, slot_acc = refs[2 * halves :]
    grads = grad_ref[...]
    gate_acc = None
    at = 0
    def hidden_part(ref, axis, begin):
        return ref[begin : begin + tile, :] if axis == 0 else ref[:, begin : begin + tile]

    for first_ref, second_ref, way in zip(first_refs, second_refs, ways):
        straight = way == NN
        for begin in range(0, second_ref.shape[1 if straight else 0], tile):
            second = hidden_part(second_ref, 1 if straight else 0, begin)
            back = lax.dot_general(grads, second, way, preferred_element_type=F32)
            product = active_ref[:, at : at + tile].astype(F32) * back
            for lane in range(0, tile, LANES):
                piece = product[:, lane : lane + LANES]
                gate_acc = piece if gate_acc is None else gate_acc + piece
            pre = (back * slope_ref[:, at : at + tile].astype(F32)).astype(BF16)
            first = hidden_part(first_ref, 0 if straight else 1, begin)
            part = lax.dot_general(pre, first, way, preferred_element_type=F32)
            slot_acc[...] = part if at == 0 else slot_acc[...] + part
            at += tile

    pick = picked(step, u_ref.shape[0])[0]
    meta = u_ref[pick, :, width:].astype(F32)
    unit_gain = u_ref[pick, :, :width]
    gate = meta[:, experts : experts + 1] + meta[:, experts + 1 : experts + 2]
    both = meta[:, experts + 2 : experts + 3] + meta[:, experts + 3 : experts + 4]
    dots = jnp.sum(gate_acc, axis=1, keepdims=True)
    lane = lax.broadcasted_iota(jnp.int32, meta.shape, 1)
    dlogits = jnp.where(lane % HALF < experts, meta, 0.0) * (both * dots)
    high, low = split_hi_lo(dlogits)
    parts = jnp.where(lane < HALF, high, low)
    router_rows = jnp.dot(parts, router_ref[...], preferred_element_type=F32)
    result = gate * slot_acc[...] + router_rows
    out_ref[...] = result.astype(BF16)
    gain_part = jnp.sum(result * unit_gain.astype(F32), axis=0, keepdims=True) / gain_ref[...]
    router_part = lax.dot_general(parts, unit_gain, TN, preferred_element_type=F32)
    parts = [jnp.broadcast_to(gain_part, (8, width)), router_part[: sums_ref.shape[0] - 8, :]]
    for begin, part in zip((0, 8), parts):
        rows = slice(begin, begin + part.shape[0])
        sums_ref[rows, :] = sums_in[0][rows, :] + part if sums_in else part


def run_experts(
    step, stack, grad_rows, active, slope, first_parts, second_parts, router_pad, gain, sums,
    experts, tile, ways,
):
    rows = stack.shape[1]
    width, part = grad_rows.shape[1], first_parts[0].size // grad_rows.shape[1]
    halves = len(first_parts)
    return pl.pallas_call(
        functools.partial(
            expert_kernel,
            step=step, halves=halves, width=width, experts=experts, tile=tile, ways=ways,
        ),
        in_specs=whole(pltpu.VMEM, 6 + len(sums) + 2 * halves),
        out_specs=whole(pltpu.VMEM, 2),
        out_shape=[
            jax.ShapeDtypeStruct((rows, width), BF16),
            jax.ShapeDtypeStruct((8 + -(-experts // 8) * 8, width), F32),
        ],
        scratch_shapes=[pltpu.VMEM((rows, width), F32)],
        compiler_params=pltpu.CompilerParams(vmem_limit_bytes=20 * MIB),
        cost_estimate=pl.CostEstimate(
            flops=4 * rows * width * halves * part,
            bytes_accessed=4 * width * halves * part,
            transcendentals=0,
        ),
        name="expert",
    )(
        stack, grad_rows, active, slope, *first_parts, *second_parts, router_pad, gain, *sums,
    )


def token_kernel(acts_ref, gain_ref, sel_ref, ret_ref, grad_ref, *refs, step):
    earlier, out_ref = refs[:-1], refs[-1]
    micro = acts_ref.shape[0]
    pick, is_last, _ = picked(step, micro)
    values = acts_ref[pick].astype(F32)
    centred = values - jnp.mean(values, axis=-1, keepdims=True)
    inverse = lax.rsqrt(jnp.mean(centred * centred, axis=-1, keepdims=True) + 1e-06)
    unit = centred * inverse
    norm_grad = jnp.dot(sel_ref[pick], ret_ref[...], preferred_element_type=F32)
    scaled = norm_grad * gain_ref[...]
    change = inverse * (
        scaled
        - jnp.mean(scaled, axis=-1, keepdims=True)
        - unit * jnp.mean(scaled * unit, axis=-1, keepdims=True)
    )
    grad = grad_ref[...].astype(F32)
    if step == 0:
        grad = jnp.where(is_last, grad, jnp.zeros_like(grad))
    result = (grad + change).astype(BF16)
    if not earlier:
        out_ref[...] = result
        return
    sections = lax.axis_size("section")
    section = lax.axis_index("section")
    for at in range(sections):

        @pl.when(section == sections - 1 - at)
        def _(at=at):
            for m in range(micro):
                out_ref[m] = result if at + m == step else earlier[at + m][...]


def run_tokens(step, acts, gain, sel, ret, grad, earlier):
    shape = acts.shape if earlier else grad.shape
    return pl.pallas_call(
        functools.partial(token_kernel, step=step),
        in_specs=whole(pltpu.VMEM, 5 + len(earlier)),
        out_specs=pl.BlockSpec(memory_space=pltpu.VMEM),
        out_shape=jax.ShapeDtypeStruct(shape, BF16),
        compiler_params=pltpu.CompilerParams(vmem_limit_bytes=4 * MIB),
        name="token",
    )(acts, gain, sel, ret, grad, *earlier)


def rows_kernel(turned_ref, in_ref, *refs, step, cap):
    *last, grad_ref, rows_ref = refs
    micro = turned_ref.shape[0]
    pick, is_last, number = picked(step, micro)
    grad = in_ref[...]
    grad = jnp.where(jnp.logical_and(number >= 0, number < micro), grad, jnp.zeros_like(grad))
    if last:
        grad = jnp.where(is_last, last[0][step], grad)
    grad_ref[...] = grad
    rows = jnp.dot(turned_ref[pick], grad, preferred_element_type=F32)
    for j in range(rows_ref.shape[0]):
        rows_ref[j] = rows[j * cap : (j + 1) * cap].astype(BF16)


def run_rows(step, turned, incoming, last_grad, experts, cap):
    last = [last_grad] if step < last_grad.shape[0] else []
    return pl.pallas_call(
        functools.partial(rows_kernel, step=step, cap=cap),
        in_specs=whole(pltpu.VMEM, 2 + len(last)),
        out_specs=whole(pltpu.VMEM, 2),
        out_shape=[
            jax.ShapeDtypeStruct(incoming.shape, BF16),
            jax.ShapeDtypeStruct((experts, cap, incoming.shape[1]), BF16),
        ],
        compiler_params=pltpu.CompilerParams(vmem_limit_bytes=4 * MIB),
        name="rows",
    )(turned, incoming, *last)


def per_device(acts, out_grad, ln_gain, router, w_in, w_out, expert_ids, slot_ids, capacity):
    sections = lax.axis_size("section")
    cores = lax.axis_size("dp")
    micro = acts.shape[1]
    tokens = acts.shape[2]
    width = acts.shape[3]
    experts = router.shape[2]
    top = expert_ids.shape[3]
    cap = 5 * tokens * top // (4 * experts)
    all_tokens = tokens * lax.axis_size("expert") * cores
    scale = 1.0 / math.sqrt(micro * all_tokens)
    tile = min(1024, w_in.shape[3])
    acts, caps, gain = acts[0], capacity[0], ln_gain
    ids, places = jnp.swapaxes(expert_ids[0], 1, 2), jnp.swapaxes(slot_ids[0], 1, 2)
    inputs = (acts, gain, router[0].T, ids, places, caps[:, None, :])

    def both_halves(own):
        turns = [[(i, (i + by) % cores) for i in range(cores)] for by in range(1, cores)]
        return [own] + [lax.ppermute(own, "dp", pairs) for pairs in turns]

    first_parts = both_halves(w_in[0, 0])
    second_parts = both_halves(w_out[0, 0])

    sent, sel0, turned0, router_pad, first_own = run_prepare(inputs, out_grad, w_in[0, 0], (0,), cap)
    first_parts[0] = first_own
    packed0 = jnp.concatenate(exchange([sent[j, 0] for j in range(experts)]), axis=0)
    split = width + LANES
    u0, grad_rows = packed0[None, :, :split], packed0[:, split:]
    rest, sel, turned, _, second_own = run_prepare(
        inputs, None, w_out[0, 0], tuple(range(1, micro)), cap
    )
    second_parts[0] = second_own
    own_turned = [run_turn(part) for part in (first_own, second_own)]
    others, _ = lax.optimization_barrier((first_parts[1:] + second_parts[1:], own_turned))
    others = [run_turn(part) for part in others]
    first_turned = own_turned[:1] + others[: cores - 1]
    second_turned = own_turned[1:] + others[cores - 1 :]
    sel = jnp.concatenate([sel0, sel], axis=0)
    turned = jnp.concatenate([turned0, turned], axis=0)

    rows_u = u0
    sums = []
    grad = out_grad[0]
    steps = micro + sections - 1
    results = []
    down = [(i, i - 1) for i in range(1, sections)]
    swap = [(sections - 1 - i, sections - 1 - (i ^ 1)) for i in range(sections)]
    for step in range(steps):
        if step > 0:
            rows_u = stack
            single = sections % 2 == 0 and step in (1, steps - 1)
            incoming = lax.ppermute(results[-1], "section", swap if single else down)
            grad, sent = run_rows(step, turned, incoming, out_grad, experts, cap)
            grad_rows = jnp.concatenate(exchange([sent[j] for j in range(experts)]), axis=0)
        active, slope = run_hidden(step, rows_u, first_parts, tile)
        slot_rows, shared = run_experts(
            step, rows_u, grad_rows, active, slope,
            first_turned if step else own_turned[:1] + first_parts[1:],
            second_turned if step else own_turned[1:] + second_parts[1:],
            router_pad, gain, sums, experts, tile, [NN] + [NN if step else NT] * (cores - 1),
        )
        sums = [shared]
        chunks = [slot_rows[j * cap : (j + 1) * cap] for j in range(experts)]
        if step == steps - 1:
            tail = jnp.concatenate([shared[:1], shared[8 : 8 + experts]], axis=0).astype(BF16)
            tail = jnp.pad(tail, ((0, -(cap + 1 + experts) % 16), (0, 0)))
            chunks = [jnp.concatenate([chunk, tail], axis=0) for chunk in chunks]
        back = exchange(chunks, back=True)
        if step == 0:
            rest, _ = lax.optimization_barrier((rest, back[-1]))
            rest = exchange([rest[j] for j in range(experts)])
            stack = jnp.concatenate([u0, jnp.concatenate(rest, axis=1)], axis=0)
        ret = jnp.concatenate([chunk[:cap] for chunk in back], axis=0)
        earlier = results if step == steps - 1 else []
        results.append(run_tokens(step, acts, gain, sel, ret, grad, earlier))

    total = sum(chunk[cap : cap + 1 + experts].astype(F32) for chunk in back)
    shared = total
    for by in range(1, cores):
        shared = shared + lax.ppermute(total, "dp", [(i, (i + by) % cores) for i in range(cores)])
    shared = shared * scale
    return (results[-1][None], shared[:1], shared[1:].T[None])


def solution(mesh):
    return jax.shard_map(
        per_device,
        mesh=mesh,
        in_specs=(
            P("section", None, ("expert", "dp"), None),
            P(None, ("expert", "dp"), None),
            P("section", None),
            P("section", None, None),
            P("section", "expert", None, "dp"),
            P("section", "expert", "dp", None),
            P("section", None, ("expert", "dp"), None),
            P("section", None, ("expert", "dp"), None),
            P("section", None, None),
        ),
        out_specs=(
            P("section", None, ("expert", "dp"), None),
            P("section", None),
            P("section", None, None),
        ),
        check_vma=False,
    )
```

```python
import functools
import math

import jax
import jax.numpy as jnp
from jax import lax
from jax.experimental import pallas as pl
from jax.experimental.pallas import tpu as pltpu
from jax.sharding import PartitionSpec as P

GELU_C = math.sqrt(2.0 / math.pi)
LANES = 128
HALF = LANES // 2
MIB = 1024 * 1024
F32 = jnp.float32
BF16 = jnp.bfloat16
NN = (((1,), (0,)), ((), ()))
NT = (((1,), (1,)), ((), ()))
TN = (((0,), (0,)), ((), ()))


def peers(count):
    if count & (count - 1) == 0:
        return [[(i, i ^ j) for i in range(count)] for j in range(count - 1, 0, -1)]
    return [[(i, (i + j) % count) for i in range(count)] for j in range(1, count)]


def relative(ids, me, count):
    if count & (count - 1) == 0:
        away = jnp.bitwise_xor(ids, me)
        return jnp.where(away > 0, count - away, away)
    away = ids - me
    return jnp.where(away < 0, away + count, away)


def picked(step, micro):
    sections = lax.axis_size("section")
    section = lax.axis_index("section")
    number = step - (sections - 1) + section
    return jnp.clip(number, 0, micro - 1), section == sections - 1, number


def exchange(chunks, back=False):
    count = len(chunks)
    out = [chunks[0]]
    for j, pairs in enumerate(peers(count), 1):
        moved = [(b, a) for a, b in pairs] if back else pairs
        out.append(lax.ppermute(chunks[j], "expert", moved))
    return out


def split_hi_lo(values):
    hi = values.astype(BF16)
    return hi, (values - hi.astype(F32)).astype(BF16)


def whole(kind, count):
    return [pl.BlockSpec(memory_space=kind)] * count


def prepare_kernel(*refs, micros, experts, cap, with_grad, keeps):
    count = 6 + with_grad
    begin = count + keeps
    rows_ref, sel_ref, turned_ref, router_ref = refs[begin : begin + 4]
    *held, sems = refs[begin + 4 + keeps :]
    kept = [
        pltpu.make_async_copy(refs[count + i], refs[begin + 4 + i], sems.at[count + i])
        for i in range(keeps)
    ]
    sources = [refs[0].at[pl.ds(micros[0], len(micros))]] + list(refs[1:6])
    if with_grad:
        sources.append(refs[6].at[pl.ds(micros[0], len(micros))])
    copies = [
        pltpu.make_async_copy(source, to, sems.at[i])
        for i, (source, to) in enumerate(zip(sources, held))
    ]
    for copy in copies + kept:
        copy.start()
    acts_ref, gain_ref, own_router_ref, ids_ref, places_ref, caps_ref = held[:6]
    me = lax.axis_index("expert")
    tokens, width = acts_ref.shape[1:]
    slots = experts * cap
    lane = lax.broadcasted_iota(jnp.int32, (tokens, LANES), 1)
    place = lax.broadcasted_iota(jnp.int32, (slots, tokens), 0)
    across = lax.broadcasted_iota(jnp.int32, (tokens, slots), 1)
    square = [lax.broadcasted_iota(jnp.int32, (tokens, tokens), axis) for axis in (0, 1)]
    diagonal = square[0] == square[1]

    def column(row):
        spread = jnp.where(diagonal, jnp.broadcast_to(row.astype(F32), diagonal.shape), 0.0)
        return jnp.sum(spread, axis=1, keepdims=True).astype(jnp.int32)

    for copy in copies:
        copy.wait()
    name = lax.broadcasted_iota(jnp.int32, (LANES, experts), 0) % HALF
    twice = jnp.where(name == lax.broadcasted_iota(jnp.int32, name.shape, 1), 1.0, 0.0)
    router_ref[...] = jnp.dot(
        twice.astype(BF16), own_router_ref[...], preferred_element_type=F32
    ).astype(BF16)
    for at, m in enumerate(micros):
        values = acts_ref[at].astype(F32)
        centred = values - jnp.mean(values, axis=-1, keepdims=True)
        inverse = lax.rsqrt(jnp.mean(centred * centred, axis=-1, keepdims=True) + 1e-06)
        normed = (centred * inverse * gain_ref[...]).astype(BF16)
        logits = lax.dot_general(normed, router_ref[...], NT, preferred_element_type=F32)
        names = [ids_ref[m, k : k + 1, :] for k in range(2)]
        tables = [jnp.where(lane % HALF == column(name), 1.0, 0.0) for name in names]
        chosen = [0.5 * jnp.sum(table * logits, axis=1, keepdims=True) for table in tables]
        gate1 = 1.0 / (1.0 + jnp.exp(chosen[1] - chosen[0]))
        gates = [gate1, 1.0 - gate1]
        both = gates[0] * gates[1]
        pairs = [tables[0] - tables[1], tables[1] - tables[0]]
        meta_rows = sel = turned = None
        for k in range(2):
            limit = jnp.zeros(names[k].shape, jnp.int32)
            for e in range(experts):
                limit = jnp.where(names[k] == e, caps_ref[m, :, e : e + 1], limit)
            own = places_ref[m, k : k + 1, :]
            target = jnp.where(own < limit, relative(names[k], me, experts) * cap + own, -1)
            hit = jnp.where(place == target, 1.0, 0.0)
            hit_across = jnp.where(across == column(target), 1.0, 0.0)
            meta = pairs[k]
            for offset, value in enumerate(split_hi_lo(gates[k]) + split_hi_lo(both)):
                meta = jnp.where(lane == experts + offset, value.astype(F32), meta)
            part = jnp.dot(hit.astype(BF16), meta.astype(BF16), preferred_element_type=F32)
            meta_rows = part if k == 0 else meta_rows + part
            turned = hit if k == 0 else turned + hit
            sel = hit_across if k == 0 else sel + hit_across
        sel_ref[at] = sel.astype(BF16)
        turned = turned.astype(BF16)
        turned_ref[at] = turned
        rows = [jnp.dot(turned, normed, preferred_element_type=F32), meta_rows]
        if with_grad:
            grad = held[6][at]
            grad = jnp.where(picked(0, 1)[1], grad, jnp.zeros_like(grad))
            rows.append(jnp.dot(turned, grad, preferred_element_type=F32))
        begin = 0
        for piece in rows:
            end = begin + piece.shape[1]
            for j in range(experts):
                rows_ref[j, at, :, begin:end] = piece[j * cap : (j + 1) * cap].astype(BF16)
            begin = end
    for copy in kept:
        copy.wait()


def run_prepare(inputs, grad, weights, micros, cap):
    _, tokens, width = inputs[0].shape
    experts = inputs[2].shape[0]
    slots, count = experts * cap, len(micros)
    packed = width + LANES + (0 if grad is None else width)
    copied = list(inputs) + ([] if grad is None else [grad])
    taken = [
        pltpu.with_memory_space_constraint(array, pltpu.HBM) for array in copied + weights
    ]
    scratch = [pltpu.VMEM(array.shape, array.dtype) for array in copied]
    for at in (0, 6)[: 1 + (grad is not None)]:
        scratch[at] = pltpu.VMEM((count, tokens, width), BF16)
    return pl.pallas_call(
        functools.partial(
            prepare_kernel,
            micros=micros, experts=experts, cap=cap, with_grad=grad is not None,
            keeps=len(weights),
        ),
        in_specs=whole(pltpu.HBM, len(taken)),
        out_specs=whole(pltpu.VMEM, 4 + len(weights)),
        out_shape=[
            jax.ShapeDtypeStruct((experts, count, cap, packed), BF16),
            jax.ShapeDtypeStruct((count, tokens, slots), BF16),
            jax.ShapeDtypeStruct((count, slots, tokens), BF16),
            jax.ShapeDtypeStruct((LANES, width), BF16),
        ]
        + [jax.ShapeDtypeStruct(array.shape, BF16) for array in weights],
        scratch_shapes=scratch + [pltpu.SemaphoreType.DMA((len(taken),))],
        compiler_params=pltpu.CompilerParams(vmem_limit_bytes=16 * MIB),
        name="prepare",
    )(*taken)


def turn_kernel(from_ref, to_ref, *, block):
    for at in range(0, from_ref.shape[0], block):
        to_ref[:, at : at + block] = from_ref[at : at + block, :].T


def run_turn(weights):
    rows, columns = weights.shape
    return pl.pallas_call(
        functools.partial(turn_kernel, block=256),
        in_specs=whole(pltpu.VMEM, 1),
        out_specs=pl.BlockSpec(memory_space=pltpu.VMEM),
        out_shape=jax.ShapeDtypeStruct((columns, rows), BF16),
        compiler_params=pltpu.CompilerParams(vmem_limit_bytes=8 * MIB),
        cost_estimate=pl.CostEstimate(
            flops=0, bytes_accessed=4 * rows * columns, transcendentals=0
        ),
        name="turn",
    )(weights)


def hidden_kernel(u_ref, *refs, step, width, tile):
    first_refs, (active_ref, slope_ref) = refs[:-2], refs[-2:]
    rows_u = u_ref[picked(step, u_ref.shape[0])[0], :, :width]
    at = 0
    for first_ref in first_refs:
        for begin in range(0, first_ref.shape[1], tile):
            hidden = jnp.dot(
                rows_u, first_ref[:, begin : begin + tile], preferred_element_type=F32
            )
            square = hidden * hidden
            tanh_val = jnp.tanh(hidden * (GELU_C + GELU_C * 0.044715 * square))
            up = 0.5 + 0.5 * tanh_val
            active_ref[:, at : at + tile] = (hidden * up).astype(BF16)
            rise = hidden * (GELU_C + GELU_C * 3.0 * 0.044715 * square)
            slope_ref[:, at : at + tile] = (up * (1.0 + (1.0 - tanh_val) * rise)).astype(BF16)
            at += tile


def run_hidden(step, stack, first_parts, tile):
    rows = stack.shape[1]
    width, part = first_parts[0].shape
    total = len(first_parts) * part
    out = jax.ShapeDtypeStruct((rows, total), BF16)
    return pl.pallas_call(
        functools.partial(hidden_kernel, step=step, width=width, tile=tile),
        in_specs=whole(pltpu.VMEM, 1 + len(first_parts)),
        out_specs=whole(pltpu.VMEM, 2),
        out_shape=[out, out],
        compiler_params=pltpu.CompilerParams(vmem_limit_bytes=20 * MIB),
        cost_estimate=pl.CostEstimate(
            flops=2 * rows * width * total,
            bytes_accessed=2 * width * total,
            transcendentals=rows * total,
        ),
        name="hidden",
    )(stack, *first_parts)


def expert_kernel(
    u_ref, grad_ref, active_ref, slope_ref, *refs, step, halves, width, experts, tile, ways
):
    first_refs, second_refs = refs[:halves], refs[halves : 2 * halves]
    router_ref, gain_ref, *sums_in, out_ref, sums_ref, slot_acc = refs[2 * halves :]
    grads = grad_ref[...]
    gate_acc = None
    at = 0
    def hidden_part(ref, axis, begin):
        return ref[begin : begin + tile, :] if axis == 0 else ref[:, begin : begin + tile]

    for first_ref, second_ref, way in zip(first_refs, second_refs, ways):
        straight = way == NN
        for begin in range(0, second_ref.shape[1 if straight else 0], tile):
            second = hidden_part(second_ref, 1 if straight else 0, begin)
            back = lax.dot_general(grads, second, way, preferred_element_type=F32)
            product = active_ref[:, at : at + tile].astype(F32) * back
            for lane in range(0, tile, LANES):
                piece = product[:, lane : lane + LANES]
                gate_acc = piece if gate_acc is None else gate_acc + piece
            pre = (back * slope_ref[:, at : at + tile].astype(F32)).astype(BF16)
            first = hidden_part(first_ref, 0 if straight else 1, begin)
            part = lax.dot_general(pre, first, way, preferred_element_type=F32)
            slot_acc[...] = part if at == 0 else slot_acc[...] + part
            at += tile

    pick = picked(step, u_ref.shape[0])[0]
    meta = u_ref[pick, :, width:].astype(F32)
    unit_gain = u_ref[pick, :, :width]
    gate = meta[:, experts : experts + 1] + meta[:, experts + 1 : experts + 2]
    both = meta[:, experts + 2 : experts + 3] + meta[:, experts + 3 : experts + 4]
    dots = jnp.sum(gate_acc, axis=1, keepdims=True)
    lane = lax.broadcasted_iota(jnp.int32, meta.shape, 1)
    dlogits = jnp.where(lane % HALF < experts, meta, 0.0) * (both * dots)
    high, low = split_hi_lo(dlogits)
    parts = jnp.where(lane < HALF, high, low)
    router_rows = jnp.dot(parts, router_ref[...], preferred_element_type=F32)
    result = gate * slot_acc[...] + router_rows
    out_ref[...] = result.astype(BF16)
    gain_part = jnp.sum(result * unit_gain.astype(F32), axis=0, keepdims=True) / gain_ref[...]
    router_part = lax.dot_general(parts, unit_gain, TN, preferred_element_type=F32)
    parts = [jnp.broadcast_to(gain_part, (8, width)), router_part[: sums_ref.shape[0] - 8, :]]
    for begin, part in zip((0, 8), parts):
        rows = slice(begin, begin + part.shape[0])
        sums_ref[rows, :] = sums_in[0][rows, :] + part if sums_in else part


def run_experts(
    step, stack, grad_rows, active, slope, first_parts, second_parts, router_pad, gain, sums,
    experts, tile, ways,
):
    rows = stack.shape[1]
    width, part = grad_rows.shape[1], first_parts[0].size // grad_rows.shape[1]
    halves = len(first_parts)
    return pl.pallas_call(
        functools.partial(
            expert_kernel,
            step=step, halves=halves, width=width, experts=experts, tile=tile, ways=ways,
        ),
        in_specs=whole(pltpu.VMEM, 6 + len(sums) + 2 * halves),
        out_specs=whole(pltpu.VMEM, 2),
        out_shape=[
            jax.ShapeDtypeStruct((rows, width), BF16),
            jax.ShapeDtypeStruct((8 + -(-experts // 8) * 8, width), F32),
        ],
        scratch_shapes=[pltpu.VMEM((rows, width), F32)],
        compiler_params=pltpu.CompilerParams(vmem_limit_bytes=20 * MIB),
        cost_estimate=pl.CostEstimate(
            flops=4 * rows * width * halves * part,
            bytes_accessed=4 * width * halves * part,
            transcendentals=0,
        ),
        name="expert",
    )(
        stack, grad_rows, active, slope, *first_parts, *second_parts, router_pad, gain, *sums,
    )


def token_kernel(acts_ref, gain_ref, sel_ref, ret_ref, grad_ref, *refs, step):
    earlier, out_ref = refs[:-1], refs[-1]
    micro = acts_ref.shape[0]
    pick, is_last, _ = picked(step, micro)
    values = acts_ref[pick].astype(F32)
    centred = values - jnp.mean(values, axis=-1, keepdims=True)
    inverse = lax.rsqrt(jnp.mean(centred * centred, axis=-1, keepdims=True) + 1e-06)
    unit = centred * inverse
    norm_grad = jnp.dot(sel_ref[pick], ret_ref[...], preferred_element_type=F32)
    scaled = norm_grad * gain_ref[...]
    change = inverse * (
        scaled
        - jnp.mean(scaled, axis=-1, keepdims=True)
        - unit * jnp.mean(scaled * unit, axis=-1, keepdims=True)
    )
    grad = grad_ref[...].astype(F32)
    if step == 0:
        grad = jnp.where(is_last, grad, jnp.zeros_like(grad))
    result = (grad + change).astype(BF16)
    if not earlier:
        out_ref[...] = result
        return
    sections = lax.axis_size("section")
    section = lax.axis_index("section")
    for at in range(sections):

        @pl.when(section == sections - 1 - at)
        def _(at=at):
            for m in range(micro):
                out_ref[m] = result if at + m == step else earlier[at + m][...]


def run_tokens(step, acts, gain, sel, ret, grad, earlier):
    shape = acts.shape if earlier else grad.shape
    return pl.pallas_call(
        functools.partial(token_kernel, step=step),
        in_specs=whole(pltpu.VMEM, 5 + len(earlier)),
        out_specs=pl.BlockSpec(memory_space=pltpu.VMEM),
        out_shape=jax.ShapeDtypeStruct(shape, BF16),
        compiler_params=pltpu.CompilerParams(vmem_limit_bytes=4 * MIB),
        name="token",
    )(acts, gain, sel, ret, grad, *earlier)


def rows_kernel(turned_ref, in_ref, *refs, step, cap):
    *last, grad_ref, rows_ref = refs
    micro = turned_ref.shape[0]
    pick, is_last, number = picked(step, micro)
    grad = in_ref[...]
    grad = jnp.where(jnp.logical_and(number >= 0, number < micro), grad, jnp.zeros_like(grad))
    if last:
        grad = jnp.where(is_last, last[0][step], grad)
    grad_ref[...] = grad
    rows = jnp.dot(turned_ref[pick], grad, preferred_element_type=F32)
    for j in range(rows_ref.shape[0]):
        rows_ref[j] = rows[j * cap : (j + 1) * cap].astype(BF16)


def run_rows(step, turned, incoming, last_grad, experts, cap):
    last = [last_grad] if step < last_grad.shape[0] else []
    return pl.pallas_call(
        functools.partial(rows_kernel, step=step, cap=cap),
        in_specs=whole(pltpu.VMEM, 2 + len(last)),
        out_specs=whole(pltpu.VMEM, 2),
        out_shape=[
            jax.ShapeDtypeStruct(incoming.shape, BF16),
            jax.ShapeDtypeStruct((experts, cap, incoming.shape[1]), BF16),
        ],
        compiler_params=pltpu.CompilerParams(vmem_limit_bytes=4 * MIB),
        name="rows",
    )(turned, incoming, *last)


def per_device(acts, out_grad, ln_gain, router, w_in, w_out, expert_ids, slot_ids, capacity):
    sections = lax.axis_size("section")
    cores = lax.axis_size("dp")
    micro = acts.shape[1]
    tokens = acts.shape[2]
    width = acts.shape[3]
    experts = router.shape[2]
    top = expert_ids.shape[3]
    cap = 5 * tokens * top // (4 * experts)
    all_tokens = tokens * lax.axis_size("expert") * cores
    scale = 1.0 / math.sqrt(micro * all_tokens)
    tile = min(1024, w_in.shape[3])
    acts, caps, gain = acts[0], capacity[0], ln_gain
    ids, places = jnp.swapaxes(expert_ids[0], 1, 2), jnp.swapaxes(slot_ids[0], 1, 2)
    inputs = (acts, gain, router[0].T, ids, places, caps[:, None, :])

    def both_halves(own):
        turns = [[(i, (i + by) % cores) for i in range(cores)] for by in range(1, cores)]
        return [own] + [lax.ppermute(own, "dp", pairs) for pairs in turns]

    first_parts = both_halves(w_in[0, 0])
    second_parts = both_halves(w_out[0, 0])

    sent, sel0, turned0, router_pad = run_prepare(inputs, out_grad, [], (0,), cap)
    packed0 = jnp.concatenate(exchange([sent[j, 0] for j in range(experts)]), axis=0)
    split = width + LANES
    u0, grad_rows = packed0[None, :, :split], packed0[:, split:]
    rest, sel, turned, _, first_own, second_own = run_prepare(
        inputs, None, [w_in[0, 0], w_out[0, 0]], tuple(range(1, micro)), cap
    )
    first_parts[0], second_parts[0] = first_own, second_own
    own_turned = [run_turn(part) for part in (first_own, second_own)]
    others, _ = lax.optimization_barrier((first_parts[1:] + second_parts[1:], own_turned))
    others = [run_turn(part) for part in others]
    first_turned = own_turned[:1] + others[: cores - 1]
    second_turned = own_turned[1:] + others[cores - 1 :]
    sel = jnp.concatenate([sel0, sel], axis=0)
    turned = jnp.concatenate([turned0, turned], axis=0)

    rows_u = u0
    sums = []
    grad = out_grad[0]
    steps = micro + sections - 1
    results = []
    down = [(i, i - 1) for i in range(1, sections)]
    swap = [(sections - 1 - i, sections - 1 - (i ^ 1)) for i in range(sections)]
    for step in range(steps):
        if step > 0:
            rows_u = stack
            single = sections % 2 == 0 and step in (1, steps - 1)
            incoming = lax.ppermute(results[-1], "section", swap if single else down)
            grad, sent = run_rows(step, turned, incoming, out_grad, experts, cap)
            grad_rows = jnp.concatenate(exchange([sent[j] for j in range(experts)]), axis=0)
        active, slope = run_hidden(step, rows_u, first_parts, tile)
        slot_rows, shared = run_experts(
            step, rows_u, grad_rows, active, slope,
            first_turned if step else own_turned[:1] + first_parts[1:],
            second_turned if step else own_turned[1:] + second_parts[1:],
            router_pad, gain, sums, experts, tile, [NN] + [NN if step else NT] * (cores - 1),
        )
        sums = [shared]
        chunks = [slot_rows[j * cap : (j + 1) * cap] for j in range(experts)]
        if step == steps - 1:
            tail = jnp.concatenate([shared[:1], shared[8 : 8 + experts]], axis=0).astype(BF16)
            tail = jnp.pad(tail, ((0, -(cap + 1 + experts) % 16), (0, 0)))
            chunks = [jnp.concatenate([chunk, tail], axis=0) for chunk in chunks]
        back = exchange(chunks, back=True)
        if step == 0:
            rest, _ = lax.optimization_barrier((rest, back[-1]))
            rest = exchange([rest[j] for j in range(experts)])
            stack = jnp.concatenate([u0, jnp.concatenate(rest, axis=1)], axis=0)
        ret = jnp.concatenate([chunk[:cap] for chunk in back], axis=0)
        earlier = results if step == steps - 1 else []
        results.append(run_tokens(step, acts, gain, sel, ret, grad, earlier))

    total = sum(chunk[cap : cap + 1 + experts].astype(F32) for chunk in back)
    shared = total
    for by in range(1, cores):
        shared = shared + lax.ppermute(total, "dp", [(i, (i + by) % cores) for i in range(cores)])
    shared = shared * scale
    return (results[-1][None], shared[:1], shared[1:].T[None])


def solution(mesh):
    return jax.shard_map(
        per_device,
        mesh=mesh,
        in_specs=(
            P("section", None, ("expert", "dp"), None),
            P(None, ("expert", "dp"), None),
            P("section", None),
            P("section", None, None),
            P("section", "expert", None, "dp"),
            P("section", "expert", "dp", None),
            P("section", None, ("expert", "dp"), None),
            P("section", None, ("expert", "dp"), None),
            P("section", None, None),
        ),
        out_specs=(
            P("section", None, ("expert", "dp"), None),
            P("section", None),
            P("section", None, None),
        ),
        check_vma=False,
    )
```

```python
import functools
import math

import jax
import jax.numpy as jnp
from jax import lax
from jax.experimental import pallas as pl
from jax.experimental.pallas import tpu as pltpu
from jax.sharding import PartitionSpec as P

GELU_C = math.sqrt(2.0 / math.pi)
LANES = 128
HALF = LANES // 2
MIB = 1024 * 1024
F32 = jnp.float32
BF16 = jnp.bfloat16
NN = (((1,), (0,)), ((), ()))
NT = (((1,), (1,)), ((), ()))
TN = (((0,), (0,)), ((), ()))


def peers(count):
    if count & (count - 1) == 0:
        return [[(i, i ^ j) for i in range(count)] for j in range(count - 1, 0, -1)]
    return [[(i, (i + j) % count) for i in range(count)] for j in range(1, count)]


def relative(ids, me, count):
    if count & (count - 1) == 0:
        away = jnp.bitwise_xor(ids, me)
        return jnp.where(away > 0, count - away, away)
    away = ids - me
    return jnp.where(away < 0, away + count, away)


def picked(step, micro):
    sections = lax.axis_size("section")
    section = lax.axis_index("section")
    number = step - (sections - 1) + section
    return jnp.clip(number, 0, micro - 1), section == sections - 1, number


def exchange(chunks, back=False):
    count = len(chunks)
    out = [chunks[0]]
    for j, pairs in enumerate(peers(count), 1):
        moved = [(b, a) for a, b in pairs] if back else pairs
        out.append(lax.ppermute(chunks[j], "expert", moved))
    return out


def split_hi_lo(values):
    hi = values.astype(BF16)
    return hi, (values - hi.astype(F32)).astype(BF16)


def whole(kind, count):
    return [pl.BlockSpec(memory_space=kind)] * count


def prepare_kernel(*refs, micros, experts, cap, with_grad, keeps):
    count = 6 + with_grad
    begin = count + keeps
    rows_ref, sel_ref, turned_ref, router_ref = refs[begin : begin + 4]
    *held, sems = refs[begin + 4 + keeps :]
    kept = [
        pltpu.make_async_copy(refs[count + i], refs[begin + 4 + i], sems.at[count + i])
        for i in range(keeps)
    ]
    sources = [refs[0].at[pl.ds(micros[0], len(micros))]] + list(refs[1:6])
    if with_grad:
        sources.append(refs[6].at[pl.ds(micros[0], len(micros))])
    copies = [
        pltpu.make_async_copy(source, to, sems.at[i])
        for i, (source, to) in enumerate(zip(sources, held))
    ]
    for copy in copies + kept:
        copy.start()
    acts_ref, gain_ref, own_router_ref, ids_ref, places_ref, caps_ref = held[:6]
    me = lax.axis_index("expert")
    tokens, width = acts_ref.shape[1:]
    slots = experts * cap
    lane = lax.broadcasted_iota(jnp.int32, (tokens, LANES), 1)
    place = lax.broadcasted_iota(jnp.int32, (slots, tokens), 0)
    across = lax.broadcasted_iota(jnp.int32, (tokens, slots), 1)
    square = [lax.broadcasted_iota(jnp.int32, (tokens, tokens), axis) for axis in (0, 1)]
    diagonal = square[0] == square[1]

    def column(row):
        spread = jnp.where(diagonal, jnp.broadcast_to(row.astype(F32), diagonal.shape), 0.0)
        return jnp.sum(spread, axis=1, keepdims=True).astype(jnp.int32)

    for copy in copies:
        copy.wait()
    name = lax.broadcasted_iota(jnp.int32, (LANES, experts), 0) % HALF
    twice = jnp.where(name == lax.broadcasted_iota(jnp.int32, name.shape, 1), 1.0, 0.0)
    router_ref[...] = jnp.dot(
        twice.astype(BF16), own_router_ref[...], preferred_element_type=F32
    ).astype(BF16)
    for at, m in enumerate(micros):
        values = acts_ref[at].astype(F32)
        centred = values - jnp.mean(values, axis=-1, keepdims=True)
        inverse = lax.rsqrt(jnp.mean(centred * centred, axis=-1, keepdims=True) + 1e-06)
        normed = (centred * inverse * gain_ref[...]).astype(BF16)
        logits = lax.dot_general(normed, router_ref[...], NT, preferred_element_type=F32)
        names = [ids_ref[m, k : k + 1, :] for k in range(2)]
        tables = [jnp.where(lane % HALF == column(name), 1.0, 0.0) for name in names]
        chosen = [0.5 * jnp.sum(table * logits, axis=1, keepdims=True) for table in tables]
        gate1 = 1.0 / (1.0 + jnp.exp(chosen[1] - chosen[0]))
        gates = [gate1, 1.0 - gate1]
        both = gates[0] * gates[1]
        pairs = [tables[0] - tables[1], tables[1] - tables[0]]
        meta_rows = sel = turned = None
        for k in range(2):
            limit = jnp.zeros(names[k].shape, jnp.int32)
            for e in range(experts):
                limit = jnp.where(names[k] == e, caps_ref[m, :, e : e + 1], limit)
            own = places_ref[m, k : k + 1, :]
            target = jnp.where(own < limit, relative(names[k], me, experts) * cap + own, -1)
            hit = jnp.where(place == target, 1.0, 0.0)
            hit_across = jnp.where(across == column(target), 1.0, 0.0)
            meta = pairs[k]
            for offset, value in enumerate(split_hi_lo(gates[k]) + split_hi_lo(both)):
                meta = jnp.where(lane == experts + offset, value.astype(F32), meta)
            part = jnp.dot(hit.astype(BF16), meta.astype(BF16), preferred_element_type=F32)
            meta_rows = part if k == 0 else meta_rows + part
            turned = hit if k == 0 else turned + hit
            sel = hit_across if k == 0 else sel + hit_across
        sel_ref[at] = sel.astype(BF16)
        turned = turned.astype(BF16)
        turned_ref[at] = turned
        rows = [jnp.dot(turned, normed, preferred_element_type=F32), meta_rows]
        if with_grad:
            grad = held[6][at]
            grad = jnp.where(picked(0, 1)[1], grad, jnp.zeros_like(grad))
            rows.append(jnp.dot(turned, grad, preferred_element_type=F32))
        begin = 0
        for piece in rows:
            end = begin + piece.shape[1]
            for j in range(experts):
                rows_ref[j, at, :, begin:end] = piece[j * cap : (j + 1) * cap].astype(BF16)
            begin = end
    for copy in kept:
        copy.wait()


def run_prepare(inputs, grad, weights, micros, cap):
    _, tokens, width = inputs[0].shape
    experts = inputs[2].shape[0]
    slots, count = experts * cap, len(micros)
    packed = width + LANES + (0 if grad is None else width)
    copied = list(inputs) + ([] if grad is None else [grad])
    taken = [
        pltpu.with_memory_space_constraint(array, pltpu.HBM) for array in copied + weights
    ]
    scratch = [pltpu.VMEM(array.shape, array.dtype) for array in copied]
    for at in (0, 6)[: 1 + (grad is not None)]:
        scratch[at] = pltpu.VMEM((count, tokens, width), BF16)
    return pl.pallas_call(
        functools.partial(
            prepare_kernel,
            micros=micros, experts=experts, cap=cap, with_grad=grad is not None,
            keeps=len(weights),
        ),
        in_specs=whole(pltpu.HBM, len(taken)),
        out_specs=whole(pltpu.VMEM, 4 + len(weights)),
        out_shape=[
            jax.ShapeDtypeStruct((experts, count, cap, packed), BF16),
            jax.ShapeDtypeStruct((count, tokens, slots), BF16),
            jax.ShapeDtypeStruct((count, slots, tokens), BF16),
            jax.ShapeDtypeStruct((LANES, width), BF16),
        ]
        + [jax.ShapeDtypeStruct(array.shape, BF16) for array in weights],
        scratch_shapes=scratch + [pltpu.SemaphoreType.DMA((len(taken),))],
        compiler_params=pltpu.CompilerParams(vmem_limit_bytes=16 * MIB),
        name="prepare",
    )(*taken)


def turn_kernel(from_ref, to_ref, *, block):
    for at in range(0, from_ref.shape[0], block):
        to_ref[:, at : at + block] = from_ref[at : at + block, :].T


def run_turn(weights):
    rows, columns = weights.shape
    return pl.pallas_call(
        functools.partial(turn_kernel, block=256),
        in_specs=whole(pltpu.VMEM, 1),
        out_specs=pl.BlockSpec(memory_space=pltpu.VMEM),
        out_shape=jax.ShapeDtypeStruct((columns, rows), BF16),
        compiler_params=pltpu.CompilerParams(vmem_limit_bytes=8 * MIB),
        cost_estimate=pl.CostEstimate(
            flops=0, bytes_accessed=4 * rows * columns, transcendentals=0
        ),
        name="turn",
    )(weights)


def hidden_kernel(u_ref, *refs, step, width, tile):
    first_refs, (active_ref, slope_ref) = refs[:-2], refs[-2:]
    rows_u = u_ref[picked(step, u_ref.shape[0])[0], :, :width]
    at = 0
    for first_ref in first_refs:
        for begin in range(0, first_ref.shape[1], tile):
            hidden = jnp.dot(
                rows_u, first_ref[:, begin : begin + tile], preferred_element_type=F32
            )
            square = hidden * hidden
            tanh_val = jnp.tanh(hidden * (GELU_C + GELU_C * 0.044715 * square))
            up = 0.5 + 0.5 * tanh_val
            active_ref[:, at : at + tile] = (hidden * up).astype(BF16)
            rise = hidden * (GELU_C + GELU_C * 3.0 * 0.044715 * square)
            slope_ref[:, at : at + tile] = (up * (1.0 + (1.0 - tanh_val) * rise)).astype(BF16)
            at += tile


def run_hidden(step, stack, first_parts, tile):
    rows = stack.shape[1]
    width, part = first_parts[0].shape
    total = len(first_parts) * part
    out = jax.ShapeDtypeStruct((rows, total), BF16)
    return pl.pallas_call(
        functools.partial(hidden_kernel, step=step, width=width, tile=tile),
        in_specs=whole(pltpu.VMEM, 1 + len(first_parts)),
        out_specs=whole(pltpu.VMEM, 2),
        out_shape=[out, out],
        compiler_params=pltpu.CompilerParams(vmem_limit_bytes=20 * MIB),
        cost_estimate=pl.CostEstimate(
            flops=2 * rows * width * total,
            bytes_accessed=2 * width * total,
            transcendentals=rows * total,
        ),
        name="hidden",
    )(stack, *first_parts)


def expert_kernel(
    u_ref, grad_ref, active_ref, slope_ref, *refs, step, halves, width, experts, tile, ways
):
    first_refs, second_refs = refs[:halves], refs[halves : 2 * halves]
    router_ref, gain_ref, *sums_in, out_ref, sums_ref, pre_ref = refs[2 * halves :]
    grads = grad_ref[...]
    gate_acc = None
    at = 0
    def hidden_part(ref, axis, begin):
        return ref[begin : begin + tile, :] if axis == 0 else ref[:, begin : begin + tile]

    for first_ref, second_ref, way in zip(first_refs, second_refs, ways):
        straight = way == NN
        for begin in range(0, second_ref.shape[1 if straight else 0], tile):
            second = hidden_part(second_ref, 1 if straight else 0, begin)
            back = lax.dot_general(grads, second, way, preferred_element_type=F32)
            product = active_ref[:, at : at + tile].astype(F32) * back
            for lane in range(0, tile, LANES):
                piece = product[:, lane : lane + LANES]
                gate_acc = piece if gate_acc is None else gate_acc + piece
            pre = back * slope_ref[:, at : at + tile].astype(F32)
            pre_ref[:, at : at + tile] = pre.astype(BF16)
            at += tile

    slots = None
    for half, (first_ref, way) in enumerate(zip(first_refs, ways)):
        count = at // halves
        pre = pre_ref[:, half * count : (half + 1) * count]
        part = lax.dot_general(pre, first_ref[...], way, preferred_element_type=F32)
        slots = part if half == 0 else slots + part

    pick = picked(step, u_ref.shape[0])[0]
    meta = u_ref[pick, :, width:].astype(F32)
    unit_gain = u_ref[pick, :, :width]
    gate = meta[:, experts : experts + 1] + meta[:, experts + 1 : experts + 2]
    both = meta[:, experts + 2 : experts + 3] + meta[:, experts + 3 : experts + 4]
    dots = jnp.sum(gate_acc, axis=1, keepdims=True)
    lane = lax.broadcasted_iota(jnp.int32, meta.shape, 1)
    dlogits = jnp.where(lane % HALF < experts, meta, 0.0) * (both * dots)
    high, low = split_hi_lo(dlogits)
    parts = jnp.where(lane < HALF, high, low)
    router_rows = jnp.dot(parts, router_ref[...], preferred_element_type=F32)
    result = gate * slots + router_rows
    out_ref[...] = result.astype(BF16)
    gain_part = jnp.sum(result * unit_gain.astype(F32), axis=0, keepdims=True) / gain_ref[...]
    router_part = lax.dot_general(parts, unit_gain, TN, preferred_element_type=F32)
    parts = [jnp.broadcast_to(gain_part, (8, width)), router_part[: sums_ref.shape[0] - 8, :]]
    for begin, part in zip((0, 8), parts):
        rows = slice(begin, begin + part.shape[0])
        sums_ref[rows, :] = sums_in[0][rows, :] + part if sums_in else part


def run_experts(
    step, stack, grad_rows, active, slope, first_parts, second_parts, router_pad, gain, sums,
    experts, tile, ways,
):
    rows = stack.shape[1]
    width, part = grad_rows.shape[1], first_parts[0].size // grad_rows.shape[1]
    halves = len(first_parts)
    return pl.pallas_call(
        functools.partial(
            expert_kernel,
            step=step, halves=halves, width=width, experts=experts, tile=tile, ways=ways,
        ),
        in_specs=whole(pltpu.VMEM, 6 + len(sums) + 2 * halves),
        out_specs=whole(pltpu.VMEM, 2),
        out_shape=[
            jax.ShapeDtypeStruct((rows, width), BF16),
            jax.ShapeDtypeStruct((8 + -(-experts // 8) * 8, width), F32),
        ],
        scratch_shapes=[pltpu.VMEM((rows, halves * part), BF16)],
        compiler_params=pltpu.CompilerParams(vmem_limit_bytes=20 * MIB),
        cost_estimate=pl.CostEstimate(
            flops=4 * rows * width * halves * part,
            bytes_accessed=4 * width * halves * part,
            transcendentals=0,
        ),
        name="expert",
    )(
        stack, grad_rows, active, slope, *first_parts, *second_parts, router_pad, gain, *sums,
    )


def token_kernel(acts_ref, gain_ref, sel_ref, ret_ref, grad_ref, *refs, step):
    earlier, out_ref = refs[:-1], refs[-1]
    micro = acts_ref.shape[0]
    pick, is_last, _ = picked(step, micro)
    values = acts_ref[pick].astype(F32)
    centred = values - jnp.mean(values, axis=-1, keepdims=True)
    inverse = lax.rsqrt(jnp.mean(centred * centred, axis=-1, keepdims=True) + 1e-06)
    unit = centred * inverse
    norm_grad = jnp.dot(sel_ref[pick], ret_ref[...], preferred_element_type=F32)
    scaled = norm_grad * gain_ref[...]
    change = inverse * (
        scaled
        - jnp.mean(scaled, axis=-1, keepdims=True)
        - unit * jnp.mean(scaled * unit, axis=-1, keepdims=True)
    )
    grad = grad_ref[...].astype(F32)
    if step == 0:
        grad = jnp.where(is_last, grad, jnp.zeros_like(grad))
    result = (grad + change).astype(BF16)
    if not earlier:
        out_ref[...] = result
        return
    sections = lax.axis_size("section")
    section = lax.axis_index("section")
    for at in range(sections):

        @pl.when(section == sections - 1 - at)
        def _(at=at):
            for m in range(micro):
                out_ref[m] = result if at + m == step else earlier[at + m][...]


def run_tokens(step, acts, gain, sel, ret, grad, earlier):
    shape = acts.shape if earlier else grad.shape
    return pl.pallas_call(
        functools.partial(token_kernel, step=step),
        in_specs=whole(pltpu.VMEM, 5 + len(earlier)),
        out_specs=pl.BlockSpec(memory_space=pltpu.VMEM),
        out_shape=jax.ShapeDtypeStruct(shape, BF16),
        compiler_params=pltpu.CompilerParams(vmem_limit_bytes=4 * MIB),
        name="token",
    )(acts, gain, sel, ret, grad, *earlier)


def rows_kernel(turned_ref, in_ref, *refs, step, cap):
    *last, grad_ref, rows_ref = refs
    micro = turned_ref.shape[0]
    pick, is_last, number = picked(step, micro)
    grad = in_ref[...]
    grad = jnp.where(jnp.logical_and(number >= 0, number < micro), grad, jnp.zeros_like(grad))
    if last:
        grad = jnp.where(is_last, last[0][step], grad)
    grad_ref[...] = grad
    rows = jnp.dot(turned_ref[pick], grad, preferred_element_type=F32)
    for j in range(rows_ref.shape[0]):
        rows_ref[j] = rows[j * cap : (j + 1) * cap].astype(BF16)


def run_rows(step, turned, incoming, last_grad, experts, cap):
    last = [last_grad] if step < last_grad.shape[0] else []
    return pl.pallas_call(
        functools.partial(rows_kernel, step=step, cap=cap),
        in_specs=whole(pltpu.VMEM, 2 + len(last)),
        out_specs=whole(pltpu.VMEM, 2),
        out_shape=[
            jax.ShapeDtypeStruct(incoming.shape, BF16),
            jax.ShapeDtypeStruct((experts, cap, incoming.shape[1]), BF16),
        ],
        compiler_params=pltpu.CompilerParams(vmem_limit_bytes=4 * MIB),
        name="rows",
    )(turned, incoming, *last)


def finish_kernel(*refs, scale):
    *part_refs, gain_ref, router_ref = refs
    total = part_refs[0][...]
    for part_ref in part_refs[1:]:
        total = total + part_ref[...]
    total = total * scale
    gain_ref[...] = total[:1]
    router_ref[...] = total[1:]


def run_finish(parts, scale):
    rows, width = parts[0].shape
    return pl.pallas_call(
        functools.partial(finish_kernel, scale=scale),
        in_specs=whole(pltpu.VMEM, len(parts)),
        out_specs=whole(pltpu.VMEM, 2),
        out_shape=[
            jax.ShapeDtypeStruct((1, width), F32),
            jax.ShapeDtypeStruct((rows - 1, width), F32),
        ],
        compiler_params=pltpu.CompilerParams(vmem_limit_bytes=4 * MIB),
        name="finish",
    )(*parts)


def per_device(acts, out_grad, ln_gain, router, w_in, w_out, expert_ids, slot_ids, capacity):
    sections = lax.axis_size("section")
    cores = lax.axis_size("dp")
    micro = acts.shape[1]
    tokens = acts.shape[2]
    width = acts.shape[3]
    experts = router.shape[2]
    top = expert_ids.shape[3]
    cap = 5 * tokens * top // (4 * experts)
    all_tokens = tokens * lax.axis_size("expert") * cores
    scale = 1.0 / math.sqrt(micro * all_tokens)
    tile = min(1024, w_in.shape[3])
    acts, caps, gain = acts[0], capacity[0], ln_gain
    ids, places = jnp.swapaxes(expert_ids[0], 1, 2), jnp.swapaxes(slot_ids[0], 1, 2)
    inputs = (acts, gain, router[0].T, ids, places, caps[:, None, :])

    def both_halves(own):
        turns = [[(i, (i + by) % cores) for i in range(cores)] for by in range(1, cores)]
        return [own] + [lax.ppermute(own, "dp", pairs) for pairs in turns]

    first_parts = both_halves(w_in[0, 0])
    second_parts = both_halves(w_out[0, 0])

    sent, sel0, turned0, router_pad = run_prepare(inputs, out_grad, [], (0,), cap)
    packed0 = jnp.concatenate(exchange([sent[j, 0] for j in range(experts)]), axis=0)
    split = width + LANES
    u0, grad_rows = packed0[None, :, :split], packed0[:, split:]
    rest, sel, turned, _, first_own, second_own = run_prepare(
        inputs, None, [w_in[0, 0], w_out[0, 0]], tuple(range(1, micro)), cap
    )
    first_parts[0], second_parts[0] = first_own, second_own
    own_turned = [run_turn(part) for part in (first_own, second_own)]
    others, _ = lax.optimization_barrier((first_parts[1:] + second_parts[1:], own_turned))
    others = [run_turn(part) for part in others]
    first_turned = own_turned[:1] + others[: cores - 1]
    second_turned = own_turned[1:] + others[cores - 1 :]
    sel = jnp.concatenate([sel0, sel], axis=0)
    turned = jnp.concatenate([turned0, turned], axis=0)

    rows_u = u0
    sums = []
    grad = out_grad[0]
    steps = micro + sections - 1
    results = []
    down = [(i, i - 1) for i in range(1, sections)]
    swap = [(sections - 1 - i, sections - 1 - (i ^ 1)) for i in range(sections)]
    for step in range(steps):
        if step > 0:
            rows_u = stack
            single = sections % 2 == 0 and step in (1, steps - 1)
            ring = down + [(0, sections - 1)]
            chain = ring if step >= micro else down
            incoming = lax.ppermute(results[-1], "section", swap if single else chain)
            grad, sent = run_rows(step, turned, incoming, out_grad, experts, cap)
            grad_rows = jnp.concatenate(exchange([sent[j] for j in range(experts)]), axis=0)
        active, slope = run_hidden(step, rows_u, first_parts, tile)
        slot_rows, shared = run_experts(
            step, rows_u, grad_rows, active, slope,
            first_turned if step else own_turned[:1] + first_parts[1:],
            second_turned if step else own_turned[1:] + second_parts[1:],
            router_pad, gain, sums, experts, tile, [NN] + [NN if step else NT] * (cores - 1),
        )
        sums = [shared]
        chunks = [slot_rows[j * cap : (j + 1) * cap] for j in range(experts)]
        if step == steps - 1:
            tail = jnp.concatenate([shared[:1], shared[8 : 8 + experts]], axis=0).astype(BF16)
            tail = jnp.pad(tail, ((0, -(cap + 1 + experts) % 16), (0, 0)))
            chunks = [jnp.concatenate([chunk, tail], axis=0) for chunk in chunks]
        back = exchange(chunks, back=True)
        if step == 0:
            rest, _ = lax.optimization_barrier((rest, back[-1]))
            rest = exchange([rest[j] for j in range(experts)])
            stack = jnp.concatenate([u0, jnp.concatenate(rest, axis=1)], axis=0)
        ret = jnp.concatenate([chunk[:cap] for chunk in back], axis=0)
        earlier = results if step == steps - 1 else []
        results.append(run_tokens(step, acts, gain, sel, ret, grad, earlier))

    total = sum(chunk[cap : cap + 1 + experts].astype(F32) for chunk in back)
    parts = [total]
    for by in range(1, cores):
        parts.append(lax.ppermute(total, "dp", [(i, (i + by) % cores) for i in range(cores)]))
    gain_grad, router_grad = run_finish(parts, scale)
    return (results[-1][None], gain_grad, router_grad.T[None])


def solution(mesh):
    return jax.shard_map(
        per_device,
        mesh=mesh,
        in_specs=(
            P("section", None, ("expert", "dp"), None),
            P(None, ("expert", "dp"), None),
            P("section", None),
            P("section", None, None),
            P("section", "expert", None, "dp"),
            P("section", "expert", "dp", None),
            P("section", None, ("expert", "dp"), None),
            P("section", None, ("expert", "dp"), None),
            P("section", None, None),
        ),
        out_specs=(
            P("section", None, ("expert", "dp"), None),
            P("section", None),
            P("section", None, None),
        ),
        check_vma=False,
    )
```

```python
import functools
import math

import jax
import jax.numpy as jnp
from jax import lax
from jax.experimental import pallas as pl
from jax.experimental.pallas import tpu as pltpu
from jax.sharding import PartitionSpec as P

GELU_C = math.sqrt(2.0 / math.pi)
LANES = 128
HALF = LANES // 2
MIB = 1024 * 1024
F32 = jnp.float32
BF16 = jnp.bfloat16
NN = (((1,), (0,)), ((), ()))
NT = (((1,), (1,)), ((), ()))
TN = (((0,), (0,)), ((), ()))


def peers(count):
    if count & (count - 1) == 0:
        return [[(i, i ^ j) for i in range(count)] for j in range(count - 1, 0, -1)]
    return [[(i, (i + j) % count) for i in range(count)] for j in range(1, count)]


def relative(ids, me, count):
    if count & (count - 1) == 0:
        away = jnp.bitwise_xor(ids, me)
        return jnp.where(away > 0, count - away, away)
    away = ids - me
    return jnp.where(away < 0, away + count, away)


def picked(step, micro):
    sections = lax.axis_size("section")
    section = lax.axis_index("section")
    number = step - (sections - 1) + section
    return jnp.clip(number, 0, micro - 1), section == sections - 1, number


def exchange(chunks, back=False):
    count = len(chunks)
    out = [chunks[0]]
    for j, pairs in enumerate(peers(count), 1):
        moved = [(b, a) for a, b in pairs] if back else pairs
        out.append(lax.ppermute(chunks[j], "expert", moved))
    return out


def split_hi_lo(values):
    hi = values.astype(BF16)
    return hi, (values - hi.astype(F32)).astype(BF16)


def whole(kind, count):
    return [pl.BlockSpec(memory_space=kind)] * count


def prepare_kernel(*refs, micros, experts, cap, with_grad, keeps):
    count = 6 + with_grad
    begin = count + keeps
    rows_ref, sel_ref, turned_ref, router_ref = refs[begin : begin + 4]
    *held, sems = refs[begin + 4 + keeps :]
    kept = [
        pltpu.make_async_copy(refs[count + i], refs[begin + 4 + i], sems.at[count + i])
        for i in range(keeps)
    ]
    sources = [refs[0].at[pl.ds(micros[0], len(micros))]] + list(refs[1:6])
    if with_grad:
        sources.append(refs[6].at[pl.ds(micros[0], len(micros))])
    copies = [
        pltpu.make_async_copy(source, to, sems.at[i])
        for i, (source, to) in enumerate(zip(sources, held))
    ]
    for copy in copies + kept:
        copy.start()
    acts_ref, gain_ref, own_router_ref, ids_ref, places_ref, caps_ref = held[:6]
    me = lax.axis_index("expert")
    tokens, width = acts_ref.shape[1:]
    slots = experts * cap
    lane = lax.broadcasted_iota(jnp.int32, (tokens, LANES), 1)
    place = lax.broadcasted_iota(jnp.int32, (slots, tokens), 0)
    across = lax.broadcasted_iota(jnp.int32, (tokens, slots), 1)
    square = [lax.broadcasted_iota(jnp.int32, (tokens, tokens), axis) for axis in (0, 1)]
    diagonal = square[0] == square[1]

    def column(row):
        spread = jnp.where(diagonal, jnp.broadcast_to(row.astype(F32), diagonal.shape), 0.0)
        return jnp.sum(spread, axis=1, keepdims=True).astype(jnp.int32)

    for copy in copies:
        copy.wait()
    name = lax.broadcasted_iota(jnp.int32, (LANES, experts), 0) % HALF
    twice = jnp.where(name == lax.broadcasted_iota(jnp.int32, name.shape, 1), 1.0, 0.0)
    router_ref[...] = jnp.dot(
        twice.astype(BF16), own_router_ref[...], preferred_element_type=F32
    ).astype(BF16)
    for at, m in enumerate(micros):
        values = acts_ref[at].astype(F32)
        centred = values - jnp.mean(values, axis=-1, keepdims=True)
        inverse = lax.rsqrt(jnp.mean(centred * centred, axis=-1, keepdims=True) + 1e-06)
        normed = (centred * inverse * gain_ref[...]).astype(BF16)
        logits = lax.dot_general(normed, router_ref[...], NT, preferred_element_type=F32)
        names = [ids_ref[m, k : k + 1, :] for k in range(2)]
        tables = [jnp.where(lane % HALF == column(name), 1.0, 0.0) for name in names]
        chosen = [0.5 * jnp.sum(table * logits, axis=1, keepdims=True) for table in tables]
        gate1 = 1.0 / (1.0 + jnp.exp(chosen[1] - chosen[0]))
        gates = [gate1, 1.0 - gate1]
        both = gates[0] * gates[1]
        pairs = [tables[0] - tables[1], tables[1] - tables[0]]
        meta_rows = sel = turned = None
        for k in range(2):
            limit = jnp.zeros(names[k].shape, jnp.int32)
            for e in range(experts):
                limit = jnp.where(names[k] == e, caps_ref[m, :, e : e + 1], limit)
            own = places_ref[m, k : k + 1, :]
            target = jnp.where(own < limit, relative(names[k], me, experts) * cap + own, -1)
            hit = jnp.where(place == target, 1.0, 0.0)
            hit_across = jnp.where(across == column(target), 1.0, 0.0)
            meta = pairs[k]
            for offset, value in enumerate(split_hi_lo(gates[k]) + split_hi_lo(both)):
                meta = jnp.where(lane == experts + offset, value.astype(F32), meta)
            part = jnp.dot(hit.astype(BF16), meta.astype(BF16), preferred_element_type=F32)
            meta_rows = part if k == 0 else meta_rows + part
            turned = hit if k == 0 else turned + hit
            sel = hit_across if k == 0 else sel + hit_across
        sel_ref[at] = sel.astype(BF16)
        turned = turned.astype(BF16)
        turned_ref[at] = turned
        rows = [jnp.dot(turned, normed, preferred_element_type=F32), meta_rows]
        if with_grad:
            grad = held[6][at]
            grad = jnp.where(picked(0, 1)[1], grad, jnp.zeros_like(grad))
            rows.append(jnp.dot(turned, grad, preferred_element_type=F32))
        begin = 0
        for piece in rows:
            end = begin + piece.shape[1]
            for j in range(experts):
                rows_ref[j, at, :, begin:end] = piece[j * cap : (j + 1) * cap].astype(BF16)
            begin = end
    for copy in kept:
        copy.wait()


def run_prepare(inputs, grad, weights, micros, cap):
    _, tokens, width = inputs[0].shape
    experts = inputs[2].shape[0]
    slots, count = experts * cap, len(micros)
    packed = width + LANES + (0 if grad is None else width)
    copied = list(inputs) + ([] if grad is None else [grad])
    taken = [
        pltpu.with_memory_space_constraint(array, pltpu.HBM) for array in copied + weights
    ]
    scratch = [pltpu.VMEM(array.shape, array.dtype) for array in copied]
    for at in (0, 6)[: 1 + (grad is not None)]:
        scratch[at] = pltpu.VMEM((count, tokens, width), BF16)
    return pl.pallas_call(
        functools.partial(
            prepare_kernel,
            micros=micros, experts=experts, cap=cap, with_grad=grad is not None,
            keeps=len(weights),
        ),
        in_specs=whole(pltpu.HBM, len(taken)),
        out_specs=whole(pltpu.VMEM, 4 + len(weights)),
        out_shape=[
            jax.ShapeDtypeStruct((experts, count, cap, packed), BF16),
            jax.ShapeDtypeStruct((count, tokens, slots), BF16),
            jax.ShapeDtypeStruct((count, slots, tokens), BF16),
            jax.ShapeDtypeStruct((LANES, width), BF16),
        ]
        + [jax.ShapeDtypeStruct(array.shape, BF16) for array in weights],
        scratch_shapes=scratch + [pltpu.SemaphoreType.DMA((len(taken),))],
        compiler_params=pltpu.CompilerParams(vmem_limit_bytes=16 * MIB),
        name="prepare",
    )(*taken)


def turn_kernel(from_ref, to_ref, *, block):
    @pl.loop(0, from_ref.shape[0] // block)
    def _(index):
        part = pl.ds(pl.multiple_of(index * block, block), block)
        to_ref[:, part] = from_ref[part, :].T


def run_turn(weights):
    rows, columns = weights.shape
    return pl.pallas_call(
        functools.partial(turn_kernel, block=256),
        in_specs=whole(pltpu.VMEM, 1),
        out_specs=pl.BlockSpec(memory_space=pltpu.VMEM),
        out_shape=jax.ShapeDtypeStruct((columns, rows), BF16),
        compiler_params=pltpu.CompilerParams(vmem_limit_bytes=8 * MIB),
        cost_estimate=pl.CostEstimate(
            flops=0, bytes_accessed=4 * rows * columns, transcendentals=0
        ),
        name="turn",
    )(weights)


def hidden_kernel(u_ref, *refs, step, width, tile):
    first_refs, (active_ref, slope_ref) = refs[:-2], refs[-2:]
    rows_u = u_ref[picked(step, u_ref.shape[0])[0], :, :width]
    part = first_refs[0].shape[1]
    for half, first_ref in enumerate(first_refs):

        @pl.loop(0, part // tile)
        def _(index, half=half, first_ref=first_ref):
            begin = pl.multiple_of(index * tile, tile)
            hidden = jnp.dot(rows_u, first_ref[:, pl.ds(begin, tile)], preferred_element_type=F32)
            square = hidden * hidden
            tanh_val = jnp.tanh(hidden * (GELU_C + GELU_C * 0.044715 * square))
            up = 0.5 + 0.5 * tanh_val
            place = pl.ds(pl.multiple_of(half * part + begin, tile), tile)
            active_ref[:, place] = (hidden * up).astype(BF16)
            rise = hidden * (GELU_C + GELU_C * 3.0 * 0.044715 * square)
            slope_ref[:, place] = (up * (1.0 + (1.0 - tanh_val) * rise)).astype(BF16)


def run_hidden(step, stack, first_parts, tile):
    rows = stack.shape[1]
    width, part = first_parts[0].shape
    total = len(first_parts) * part
    out = jax.ShapeDtypeStruct((rows, total), BF16)
    return pl.pallas_call(
        functools.partial(hidden_kernel, step=step, width=width, tile=tile),
        in_specs=whole(pltpu.VMEM, 1 + len(first_parts)),
        out_specs=whole(pltpu.VMEM, 2),
        out_shape=[out, out],
        compiler_params=pltpu.CompilerParams(vmem_limit_bytes=20 * MIB),
        cost_estimate=pl.CostEstimate(
            flops=2 * rows * width * total,
            bytes_accessed=2 * width * total,
            transcendentals=rows * total,
        ),
        name="hidden",
    )(stack, *first_parts)


def expert_kernel(
    u_ref, grad_ref, active_ref, slope_ref, *refs, step, halves, width, experts, tile, ways
):
    first_refs, second_refs = refs[:halves], refs[halves : 2 * halves]
    router_ref, gain_ref, *sums_in, out_ref, sums_ref, pre_ref = refs[2 * halves :]
    grads = grad_ref[...]
    gate_acc = None
    at = 0
    def hidden_part(ref, axis, begin):
        return ref[begin : begin + tile, :] if axis == 0 else ref[:, begin : begin + tile]

    for first_ref, second_ref, way in zip(first_refs, second_refs, ways):
        straight = way == NN
        for begin in range(0, second_ref.shape[1 if straight else 0], tile):
            second = hidden_part(second_ref, 1 if straight else 0, begin)
            back = lax.dot_general(grads, second, way, preferred_element_type=F32)
            product = active_ref[:, at : at + tile].astype(F32) * back
            for lane in range(0, tile, LANES):
                piece = product[:, lane : lane + LANES]
                gate_acc = piece if gate_acc is None else gate_acc + piece
            pre = back * slope_ref[:, at : at + tile].astype(F32)
            pre_ref[:, at : at + tile] = pre.astype(BF16)
            at += tile

    slots = None
    for half, (first_ref, way) in enumerate(zip(first_refs, ways)):
        count = at // halves
        pre = pre_ref[:, half * count : (half + 1) * count]
        part = lax.dot_general(pre, first_ref[...], way, preferred_element_type=F32)
        slots = part if half == 0 else slots + part

    pick = picked(step, u_ref.shape[0])[0]
    meta = u_ref[pick, :, width:].astype(F32)
    unit_gain = u_ref[pick, :, :width]
    gate = meta[:, experts : experts + 1] + meta[:, experts + 1 : experts + 2]
    both = meta[:, experts + 2 : experts + 3] + meta[:, experts + 3 : experts + 4]
    dots = jnp.sum(gate_acc, axis=1, keepdims=True)
    lane = lax.broadcasted_iota(jnp.int32, meta.shape, 1)
    dlogits = jnp.where(lane % HALF < experts, meta, 0.0) * (both * dots)
    high, low = split_hi_lo(dlogits)
    parts = jnp.where(lane < HALF, high, low)
    router_rows = jnp.dot(parts, router_ref[...], preferred_element_type=F32)
    result = gate * slots + router_rows
    out_ref[...] = result.astype(BF16)
    gain_part = jnp.sum(result * unit_gain.astype(F32), axis=0, keepdims=True) / gain_ref[...]
    router_part = lax.dot_general(parts, unit_gain, TN, preferred_element_type=F32)
    parts = [jnp.broadcast_to(gain_part, (8, width)), router_part[: sums_ref.shape[0] - 8, :]]
    for begin, part in zip((0, 8), parts):
        rows = slice(begin, begin + part.shape[0])
        sums_ref[rows, :] = sums_in[0][rows, :] + part if sums_in else part


def run_experts(
    step, stack, grad_rows, active, slope, first_parts, second_parts, router_pad, gain, sums,
    experts, tile, ways,
):
    rows = stack.shape[1]
    width, part = grad_rows.shape[1], first_parts[0].size // grad_rows.shape[1]
    halves = len(first_parts)
    return pl.pallas_call(
        functools.partial(
            expert_kernel,
            step=step, halves=halves, width=width, experts=experts, tile=tile, ways=ways,
        ),
        in_specs=whole(pltpu.VMEM, 6 + len(sums) + 2 * halves),
        out_specs=whole(pltpu.VMEM, 2),
        out_shape=[
            jax.ShapeDtypeStruct((rows, width), BF16),
            jax.ShapeDtypeStruct((8 + -(-experts // 8) * 8, width), F32),
        ],
        scratch_shapes=[pltpu.VMEM((rows, halves * part), BF16)],
        compiler_params=pltpu.CompilerParams(vmem_limit_bytes=20 * MIB),
        cost_estimate=pl.CostEstimate(
            flops=4 * rows * width * halves * part,
            bytes_accessed=4 * width * halves * part,
            transcendentals=0,
        ),
        name="expert",
    )(
        stack, grad_rows, active, slope, *first_parts, *second_parts, router_pad, gain, *sums,
    )


def token_kernel(acts_ref, gain_ref, sel_ref, ret_ref, grad_ref, *refs, step):
    earlier, out_ref = refs[:-1], refs[-1]
    micro = acts_ref.shape[0]
    pick, is_last, _ = picked(step, micro)
    values = acts_ref[pick].astype(F32)
    centred = values - jnp.mean(values, axis=-1, keepdims=True)
    inverse = lax.rsqrt(jnp.mean(centred * centred, axis=-1, keepdims=True) + 1e-06)
    unit = centred * inverse
    norm_grad = jnp.dot(sel_ref[pick], ret_ref[...], preferred_element_type=F32)
    scaled = norm_grad * gain_ref[...]
    change = inverse * (
        scaled
        - jnp.mean(scaled, axis=-1, keepdims=True)
        - unit * jnp.mean(scaled * unit, axis=-1, keepdims=True)
    )
    grad = grad_ref[...].astype(F32)
    if step == 0:
        grad = jnp.where(is_last, grad, jnp.zeros_like(grad))
    result = (grad + change).astype(BF16)
    if not earlier:
        out_ref[...] = result
        return
    sections = lax.axis_size("section")
    section = lax.axis_index("section")
    for at in range(sections):

        @pl.when(section == sections - 1 - at)
        def _(at=at):
            for m in range(micro):
                out_ref[m] = result if at + m == step else earlier[at + m][...]


def run_tokens(step, acts, gain, sel, ret, grad, earlier):
    shape = acts.shape if earlier else grad.shape
    return pl.pallas_call(
        functools.partial(token_kernel, step=step),
        in_specs=whole(pltpu.VMEM, 5 + len(earlier)),
        out_specs=pl.BlockSpec(memory_space=pltpu.VMEM),
        out_shape=jax.ShapeDtypeStruct(shape, BF16),
        compiler_params=pltpu.CompilerParams(vmem_limit_bytes=4 * MIB),
        name="token",
    )(acts, gain, sel, ret, grad, *earlier)


def rows_kernel(turned_ref, in_ref, *refs, step, cap):
    *last, grad_ref, rows_ref = refs
    micro = turned_ref.shape[0]
    pick, is_last, number = picked(step, micro)
    grad = in_ref[...]
    grad = jnp.where(jnp.logical_and(number >= 0, number < micro), grad, jnp.zeros_like(grad))
    if last:
        grad = jnp.where(is_last, last[0][step], grad)
    grad_ref[...] = grad
    rows = jnp.dot(turned_ref[pick], grad, preferred_element_type=F32)
    for j in range(rows_ref.shape[0]):
        rows_ref[j] = rows[j * cap : (j + 1) * cap].astype(BF16)


def run_rows(step, turned, incoming, last_grad, experts, cap):
    last = [last_grad] if step < last_grad.shape[0] else []
    return pl.pallas_call(
        functools.partial(rows_kernel, step=step, cap=cap),
        in_specs=whole(pltpu.VMEM, 2 + len(last)),
        out_specs=whole(pltpu.VMEM, 2),
        out_shape=[
            jax.ShapeDtypeStruct(incoming.shape, BF16),
            jax.ShapeDtypeStruct((experts, cap, incoming.shape[1]), BF16),
        ],
        compiler_params=pltpu.CompilerParams(vmem_limit_bytes=4 * MIB),
        name="rows",
    )(turned, incoming, *last)


def finish_kernel(*refs, scale):
    *part_refs, gain_ref, router_ref = refs
    total = part_refs[0][...]
    for part_ref in part_refs[1:]:
        total = total + part_ref[...]
    total = total * scale
    gain_ref[...] = total[:1]
    router_ref[...] = total[1:]


def run_finish(parts, scale):
    rows, width = parts[0].shape
    return pl.pallas_call(
        functools.partial(finish_kernel, scale=scale),
        in_specs=whole(pltpu.VMEM, len(parts)),
        out_specs=whole(pltpu.VMEM, 2),
        out_shape=[
            jax.ShapeDtypeStruct((1, width), F32),
            jax.ShapeDtypeStruct((rows - 1, width), F32),
        ],
        compiler_params=pltpu.CompilerParams(vmem_limit_bytes=4 * MIB),
        name="finish",
    )(*parts)


def per_device(acts, out_grad, ln_gain, router, w_in, w_out, expert_ids, slot_ids, capacity):
    sections = lax.axis_size("section")
    cores = lax.axis_size("dp")
    micro = acts.shape[1]
    tokens = acts.shape[2]
    width = acts.shape[3]
    experts = router.shape[2]
    top = expert_ids.shape[3]
    cap = 5 * tokens * top // (4 * experts)
    all_tokens = tokens * lax.axis_size("expert") * cores
    scale = 1.0 / math.sqrt(micro * all_tokens)
    tile = min(1024, w_in.shape[3])
    acts, caps, gain = acts[0], capacity[0], ln_gain
    ids, places = jnp.swapaxes(expert_ids[0], 1, 2), jnp.swapaxes(slot_ids[0], 1, 2)
    inputs = (acts, gain, router[0].T, ids, places, caps[:, None, :])

    def both_halves(own):
        turns = [[(i, (i + by) % cores) for i in range(cores)] for by in range(1, cores)]
        return [own] + [lax.ppermute(own, "dp", pairs) for pairs in turns]

    first_parts = both_halves(w_in[0, 0])
    second_parts = both_halves(w_out[0, 0])

    sent, sel0, turned0, router_pad = run_prepare(inputs, out_grad, [], (0,), cap)
    packed0 = jnp.concatenate(exchange([sent[j, 0] for j in range(experts)]), axis=0)
    split = width + LANES
    u0, grad_rows = packed0[None, :, :split], packed0[:, split:]
    rest, sel, turned, _, first_own, second_own = run_prepare(
        inputs, None, [w_in[0, 0], w_out[0, 0]], tuple(range(1, micro)), cap
    )
    first_parts[0], second_parts[0] = first_own, second_own
    own_turned = [run_turn(part) for part in (first_own, second_own)]
    others, _ = lax.optimization_barrier((first_parts[1:] + second_parts[1:], own_turned))
    others = [run_turn(part) for part in others]
    first_turned = own_turned[:1] + others[: cores - 1]
    second_turned = own_turned[1:] + others[cores - 1 :]
    sel = jnp.concatenate([sel0, sel], axis=0)
    turned = jnp.concatenate([turned0, turned], axis=0)

    rows_u = u0
    sums = []
    grad = out_grad[0]
    steps = micro + sections - 1
    results = []
    down = [(i, i - 1) for i in range(1, sections)]
    swap = [(sections - 1 - i, sections - 1 - (i ^ 1)) for i in range(sections)]
    for step in range(steps):
        if step > 0:
            rows_u = stack
            single = sections % 2 == 0 and step in (1, steps - 1)
            ring = down + [(0, sections - 1)]
            chain = ring if step >= micro else down
            incoming = lax.ppermute(results[-1], "section", swap if single else chain)
            grad, sent = run_rows(step, turned, incoming, out_grad, experts, cap)
            grad_rows = jnp.concatenate(exchange([sent[j] for j in range(experts)]), axis=0)
        active, slope = run_hidden(step, rows_u, first_parts, tile)
        slot_rows, shared = run_experts(
            step, rows_u, grad_rows, active, slope,
            first_turned if step else own_turned[:1] + first_parts[1:],
            second_turned if step else own_turned[1:] + second_parts[1:],
            router_pad, gain, sums, experts, tile, [NN] + [NN if step else NT] * (cores - 1),
        )
        sums = [shared]
        chunks = [slot_rows[j * cap : (j + 1) * cap] for j in range(experts)]
        if step == steps - 1:
            tail = jnp.concatenate([shared[:1], shared[8 : 8 + experts]], axis=0).astype(BF16)
            tail = jnp.pad(tail, ((0, -(cap + 1 + experts) % 16), (0, 0)))
            chunks = [jnp.concatenate([chunk, tail], axis=0) for chunk in chunks]
        back = exchange(chunks, back=True)
        if step == 0:
            rest, _ = lax.optimization_barrier((rest, back[-1]))
            rest = exchange([rest[j] for j in range(experts)])
            stack = jnp.concatenate([u0, jnp.concatenate(rest, axis=1)], axis=0)
        ret = jnp.concatenate([chunk[:cap] for chunk in back], axis=0)
        earlier = results if step == steps - 1 else []
        results.append(run_tokens(step, acts, gain, sel, ret, grad, earlier))

    total = sum(chunk[cap : cap + 1 + experts].astype(F32) for chunk in back)
    parts = [total]
    for by in range(1, cores):
        parts.append(lax.ppermute(total, "dp", [(i, (i + by) % cores) for i in range(cores)]))
    gain_grad, router_grad = run_finish(parts, scale)
    return (results[-1][None], gain_grad, router_grad.T[None])


def solution(mesh):
    return jax.shard_map(
        per_device,
        mesh=mesh,
        in_specs=(
            P("section", None, ("expert", "dp"), None),
            P(None, ("expert", "dp"), None),
            P("section", None),
            P("section", None, None),
            P("section", "expert", None, "dp"),
            P("section", "expert", "dp", None),
            P("section", None, ("expert", "dp"), None),
            P("section", None, ("expert", "dp"), None),
            P("section", None, None),
        ),
        out_specs=(
            P("section", None, ("expert", "dp"), None),
            P("section", None),
            P("section", None, None),
        ),
        check_vma=False,
    )
```

```python
import functools
import math

import jax
import jax.numpy as jnp
from jax import lax
from jax.experimental import pallas as pl
from jax.experimental.pallas import tpu as pltpu
from jax.sharding import PartitionSpec as P

GELU_C = math.sqrt(2.0 / math.pi)
LANES = 128
HALF = LANES // 2
MIB = 1024 * 1024
F32 = jnp.float32
BF16 = jnp.bfloat16
NN = (((1,), (0,)), ((), ()))
NT = (((1,), (1,)), ((), ()))
TN = (((0,), (0,)), ((), ()))


def peers(count):
    if count & (count - 1) == 0:
        return [[(i, i ^ j) for i in range(count)] for j in range(count - 1, 0, -1)]
    return [[(i, (i + j) % count) for i in range(count)] for j in range(1, count)]


def relative(ids, me, count):
    if count & (count - 1) == 0:
        away = jnp.bitwise_xor(ids, me)
        return jnp.where(away > 0, count - away, away)
    away = ids - me
    return jnp.where(away < 0, away + count, away)


def picked(step, micro):
    sections = lax.axis_size("section")
    section = lax.axis_index("section")
    number = step - (sections - 1) + section
    return jnp.clip(number, 0, micro - 1), section == sections - 1, number


def exchange(chunks, back=False):
    count = len(chunks)
    out = [chunks[0]]
    for j, pairs in enumerate(peers(count), 1):
        moved = [(b, a) for a, b in pairs] if back else pairs
        out.append(lax.ppermute(chunks[j], "expert", moved))
    return out


def split_hi_lo(values):
    hi = values.astype(BF16)
    return hi, (values - hi.astype(F32)).astype(BF16)


def whole(kind, count):
    return [pl.BlockSpec(memory_space=kind)] * count


def prepare_kernel(*refs, micros, experts, cap, with_grad, keeps):
    count = 6 + with_grad
    begin = count + keeps
    rows_ref, turned_ref, router_ref = refs[begin : begin + 3]
    sel_ref = None if with_grad else refs[begin + 3]
    first = begin + 3 + (not with_grad)
    *held, sems = refs[first + keeps :]
    kept = [
        pltpu.make_async_copy(refs[count + i], refs[first + i], sems.at[count + i])
        for i in range(keeps)
    ]
    sources = [refs[0].at[pl.ds(micros[0], len(micros))]] + list(refs[1:6])
    if with_grad:
        sources.append(refs[6].at[pl.ds(micros[0], len(micros))])
    copies = [
        pltpu.make_async_copy(source, to, sems.at[i])
        for i, (source, to) in enumerate(zip(sources, held))
    ]
    for copy in copies + kept:
        copy.start()
    acts_ref, gain_ref, own_router_ref, ids_ref, places_ref, caps_ref = held[:6]
    me = lax.axis_index("expert")
    tokens, width = acts_ref.shape[1:]
    slots = experts * cap
    lane = lax.broadcasted_iota(jnp.int32, (tokens, LANES), 1)
    place = lax.broadcasted_iota(jnp.int32, (slots, tokens), 0)
    across = lax.broadcasted_iota(jnp.int32, (tokens, slots), 1)
    square = [lax.broadcasted_iota(jnp.int32, (tokens, tokens), axis) for axis in (0, 1)]
    diagonal = square[0] == square[1]

    def column(row):
        spread = jnp.where(diagonal, jnp.broadcast_to(row.astype(F32), diagonal.shape), 0.0)
        return jnp.sum(spread, axis=1, keepdims=True).astype(jnp.int32)

    def target_of(m, k):
        name, own = ids_ref[m, k : k + 1, :], places_ref[m, k : k + 1, :]
        limit = jnp.zeros(name.shape, jnp.int32)
        for e in range(experts):
            limit = jnp.where(name == e, caps_ref[m, :, e : e + 1], limit)
        return jnp.where(own < limit, relative(name, me, experts) * cap + own, -1)

    for copy in copies:
        copy.wait()
    name = lax.broadcasted_iota(jnp.int32, (LANES, experts), 0) % HALF
    twice = jnp.where(name == lax.broadcasted_iota(jnp.int32, name.shape, 1), 1.0, 0.0)
    router_ref[...] = jnp.dot(
        twice.astype(BF16), own_router_ref[...], preferred_element_type=F32
    ).astype(BF16)
    for at, m in enumerate(micros):
        values = acts_ref[at].astype(F32)
        centred = values - jnp.mean(values, axis=-1, keepdims=True)
        inverse = lax.rsqrt(jnp.mean(centred * centred, axis=-1, keepdims=True) + 1e-06)
        normed = (centred * inverse * gain_ref[...]).astype(BF16)
        logits = lax.dot_general(normed, router_ref[...], NT, preferred_element_type=F32)
        names = [ids_ref[m, k : k + 1, :] for k in range(2)]
        tables = [jnp.where(lane % HALF == column(name), 1.0, 0.0) for name in names]
        chosen = [0.5 * jnp.sum(table * logits, axis=1, keepdims=True) for table in tables]
        gate1 = 1.0 / (1.0 + jnp.exp(chosen[1] - chosen[0]))
        gates = [gate1, 1.0 - gate1]
        both = gates[0] * gates[1]
        pairs = [tables[0] - tables[1], tables[1] - tables[0]]
        meta_rows = turned = None
        for k in range(2):
            target = target_of(m, k)
            hit = jnp.where(place == target, 1.0, 0.0)
            meta = pairs[k]
            for offset, value in enumerate(split_hi_lo(gates[k]) + split_hi_lo(both)):
                meta = jnp.where(lane == experts + offset, value.astype(F32), meta)
            part = jnp.dot(hit.astype(BF16), meta.astype(BF16), preferred_element_type=F32)
            meta_rows = part if k == 0 else meta_rows + part
            turned = hit if k == 0 else turned + hit
        turned = turned.astype(BF16)
        turned_ref[at] = turned
        rows = [jnp.dot(turned, normed, preferred_element_type=F32), meta_rows]
        if with_grad:
            grad = held[6][at]
            grad = jnp.where(picked(0, 1)[1], grad, jnp.zeros_like(grad))
            rows.append(jnp.dot(turned, grad, preferred_element_type=F32))
        begin = 0
        for piece in rows:
            end = begin + piece.shape[1]
            for j in range(experts):
                rows_ref[j, at, :, begin:end] = piece[j * cap : (j + 1) * cap].astype(BF16)
            begin = end
    for m in range(sel_ref.shape[0] if not with_grad else 0):
        spots = [column(target_of(m, k)) for k in range(2)]
        hit = jnp.logical_or(across == spots[0], across == spots[1])
        sel_ref[m] = jnp.where(hit, 1.0, 0.0).astype(BF16)
    for copy in kept:
        copy.wait()


def run_prepare(inputs, grad, weights, micros, cap):
    _, tokens, width = inputs[0].shape
    experts = inputs[2].shape[0]
    slots, count = experts * cap, len(micros)
    packed = width + LANES + (0 if grad is None else width)
    copied = list(inputs) + ([] if grad is None else [grad])
    taken = [
        pltpu.with_memory_space_constraint(array, pltpu.HBM) for array in copied + weights
    ]
    scratch = [pltpu.VMEM(array.shape, array.dtype) for array in copied]
    for at in (0, 6)[: 1 + (grad is not None)]:
        scratch[at] = pltpu.VMEM((count, tokens, width), BF16)
    return pl.pallas_call(
        functools.partial(
            prepare_kernel,
            micros=micros, experts=experts, cap=cap, with_grad=grad is not None,
            keeps=len(weights),
        ),
        in_specs=whole(pltpu.HBM, len(taken)),
        out_specs=whole(pltpu.VMEM, 3 + (grad is None) + len(weights)),
        out_shape=[
            jax.ShapeDtypeStruct((experts, count, cap, packed), BF16),
            jax.ShapeDtypeStruct((count, slots, tokens), BF16),
            jax.ShapeDtypeStruct((LANES, width), BF16),
        ]
        + [jax.ShapeDtypeStruct((inputs[0].shape[0], tokens, slots), BF16)] * (grad is None)
        + [jax.ShapeDtypeStruct(array.shape, BF16) for array in weights],
        scratch_shapes=scratch + [pltpu.SemaphoreType.DMA((len(taken),))],
        compiler_params=pltpu.CompilerParams(vmem_limit_bytes=16 * MIB),
        name="prepare",
    )(*taken)


def turn_kernel(from_ref, to_ref, *, block):
    for at in range(0, from_ref.shape[0], block):
        to_ref[:, at : at + block] = from_ref[at : at + block, :].T


def run_turn(weights):
    rows, columns = weights.shape
    return pl.pallas_call(
        functools.partial(turn_kernel, block=256),
        in_specs=whole(pltpu.VMEM, 1),
        out_specs=pl.BlockSpec(memory_space=pltpu.VMEM),
        out_shape=jax.ShapeDtypeStruct((columns, rows), BF16),
        compiler_params=pltpu.CompilerParams(vmem_limit_bytes=8 * MIB),
        cost_estimate=pl.CostEstimate(
            flops=0, bytes_accessed=4 * rows * columns, transcendentals=0
        ),
        name="turn",
    )(weights)


def hidden_kernel(u_ref, *refs, step, width, tile):
    first_refs, (active_ref, slope_ref) = refs[:-2], refs[-2:]
    rows_u = u_ref[picked(step, u_ref.shape[0])[0], :, :width]
    at = 0
    for first_ref in first_refs:
        for begin in range(0, first_ref.shape[1], tile):
            hidden = jnp.dot(
                rows_u, first_ref[:, begin : begin + tile], preferred_element_type=F32
            )
            square = hidden * hidden
            tanh_val = jnp.tanh(hidden * (GELU_C + GELU_C * 0.044715 * square))
            up = 0.5 + 0.5 * tanh_val
            active_ref[:, at : at + tile] = (hidden * up).astype(BF16)
            rise = hidden * (GELU_C + GELU_C * 3.0 * 0.044715 * square)
            slope_ref[:, at : at + tile] = (up * (1.0 + (1.0 - tanh_val) * rise)).astype(BF16)
            at += tile


def run_hidden(step, stack, first_parts, tile):
    rows = stack.shape[1]
    width, part = first_parts[0].shape
    total = len(first_parts) * part
    out = jax.ShapeDtypeStruct((rows, total), BF16)
    return pl.pallas_call(
        functools.partial(hidden_kernel, step=step, width=width, tile=tile),
        in_specs=whole(pltpu.VMEM, 1 + len(first_parts)),
        out_specs=whole(pltpu.VMEM, 2),
        out_shape=[out, out],
        compiler_params=pltpu.CompilerParams(vmem_limit_bytes=20 * MIB),
        cost_estimate=pl.CostEstimate(
            flops=2 * rows * width * total,
            bytes_accessed=2 * width * total,
            transcendentals=rows * total,
        ),
        name="hidden",
    )(stack, *first_parts)


def expert_kernel(
    u_ref, grad_ref, active_ref, slope_ref, *refs, step, halves, width, experts, tile, ways
):
    first_refs, second_refs = refs[:halves], refs[halves : 2 * halves]
    router_ref, gain_ref, *sums_in, out_ref, sums_ref, pre_ref = refs[2 * halves :]
    grads = grad_ref[...]
    gate_acc = None
    at = 0
    def hidden_part(ref, axis, begin):
        return ref[begin : begin + tile, :] if axis == 0 else ref[:, begin : begin + tile]

    for first_ref, second_ref, way in zip(first_refs, second_refs, ways):
        straight = way == NN
        for begin in range(0, second_ref.shape[1 if straight else 0], tile):
            second = hidden_part(second_ref, 1 if straight else 0, begin)
            back = lax.dot_general(grads, second, way, preferred_element_type=F32)
            product = active_ref[:, at : at + tile].astype(F32) * back
            for lane in range(0, tile, LANES):
                piece = product[:, lane : lane + LANES]
                gate_acc = piece if gate_acc is None else gate_acc + piece
            pre = back * slope_ref[:, at : at + tile].astype(F32)
            pre_ref[:, at : at + tile] = pre.astype(BF16)
            at += tile

    slots = None
    for half, (first_ref, way) in enumerate(zip(first_refs, ways)):
        count = at // halves
        pre = pre_ref[:, half * count : (half + 1) * count]
        part = lax.dot_general(pre, first_ref[...], way, preferred_element_type=F32)
        slots = part if half == 0 else slots + part

    pick = picked(step, u_ref.shape[0])[0]
    meta = u_ref[pick, :, width:].astype(F32)
    unit_gain = u_ref[pick, :, :width]
    gate = meta[:, experts : experts + 1] + meta[:, experts + 1 : experts + 2]
    both = meta[:, experts + 2 : experts + 3] + meta[:, experts + 3 : experts + 4]
    dots = jnp.sum(gate_acc, axis=1, keepdims=True)
    lane = lax.broadcasted_iota(jnp.int32, meta.shape, 1)
    dlogits = jnp.where(lane % HALF < experts, meta, 0.0) * (both * dots)
    high, low = split_hi_lo(dlogits)
    parts = jnp.where(lane < HALF, high, low)
    router_rows = jnp.dot(parts, router_ref[...], preferred_element_type=F32)
    result = gate * slots + router_rows
    out_ref[...] = result.astype(BF16)
    gain_part = jnp.sum(result * unit_gain.astype(F32), axis=0, keepdims=True) / gain_ref[...]
    router_part = lax.dot_general(parts, unit_gain, TN, preferred_element_type=F32)
    parts = [jnp.broadcast_to(gain_part, (8, width)), router_part[: sums_ref.shape[0] - 8, :]]
    for begin, part in zip((0, 8), parts):
        rows = slice(begin, begin + part.shape[0])
        sums_ref[rows, :] = sums_in[0][rows, :] + part if sums_in else part


def run_experts(
    step, stack, grad_rows, active, slope, first_parts, second_parts, router_pad, gain, sums,
    experts, tile, ways,
):
    rows = stack.shape[1]
    width, part = grad_rows.shape[1], first_parts[0].size // grad_rows.shape[1]
    halves = len(first_parts)
    return pl.pallas_call(
        functools.partial(
            expert_kernel,
            step=step, halves=halves, width=width, experts=experts, tile=tile, ways=ways,
        ),
        in_specs=whole(pltpu.VMEM, 6 + len(sums) + 2 * halves),
        out_specs=whole(pltpu.VMEM, 2),
        out_shape=[
            jax.ShapeDtypeStruct((rows, width), BF16),
            jax.ShapeDtypeStruct((8 + -(-experts // 8) * 8, width), F32),
        ],
        scratch_shapes=[pltpu.VMEM((rows, halves * part), BF16)],
        compiler_params=pltpu.CompilerParams(vmem_limit_bytes=20 * MIB),
        cost_estimate=pl.CostEstimate(
            flops=4 * rows * width * halves * part,
            bytes_accessed=4 * width * halves * part,
            transcendentals=0,
        ),
        name="expert",
    )(
        stack, grad_rows, active, slope, *first_parts, *second_parts, router_pad, gain, *sums,
    )


def token_kernel(acts_ref, gain_ref, sel_ref, ret_ref, grad_ref, *refs, step):
    earlier, out_ref = refs[:-1], refs[-1]
    micro = acts_ref.shape[0]
    pick, is_last, _ = picked(step, micro)
    values = acts_ref[pick].astype(F32)
    centred = values - jnp.mean(values, axis=-1, keepdims=True)
    inverse = lax.rsqrt(jnp.mean(centred * centred, axis=-1, keepdims=True) + 1e-06)
    unit = centred * inverse
    norm_grad = jnp.dot(sel_ref[pick], ret_ref[...], preferred_element_type=F32)
    scaled = norm_grad * gain_ref[...]
    change = inverse * (
        scaled
        - jnp.mean(scaled, axis=-1, keepdims=True)
        - unit * jnp.mean(scaled * unit, axis=-1, keepdims=True)
    )
    grad = grad_ref[...].astype(F32)
    if step == 0:
        grad = jnp.where(is_last, grad, jnp.zeros_like(grad))
    result = (grad + change).astype(BF16)
    if not earlier:
        out_ref[...] = result
        return
    sections = lax.axis_size("section")
    section = lax.axis_index("section")
    for at in range(sections):

        @pl.when(section == sections - 1 - at)
        def _(at=at):
            for m in range(micro):
                out_ref[m] = result if at + m == step else earlier[at + m][...]


def run_tokens(step, acts, gain, sel, ret, grad, earlier):
    shape = acts.shape if earlier else grad.shape
    return pl.pallas_call(
        functools.partial(token_kernel, step=step),
        in_specs=whole(pltpu.VMEM, 5 + len(earlier)),
        out_specs=pl.BlockSpec(memory_space=pltpu.VMEM),
        out_shape=jax.ShapeDtypeStruct(shape, BF16),
        compiler_params=pltpu.CompilerParams(vmem_limit_bytes=4 * MIB),
        name="token",
    )(acts, gain, sel, ret, grad, *earlier)


def rows_kernel(turned_ref, in_ref, *refs, step, cap):
    *last, grad_ref, rows_ref = refs
    micro = turned_ref.shape[0]
    pick, is_last, number = picked(step, micro)
    grad = in_ref[...]
    grad = jnp.where(jnp.logical_and(number >= 0, number < micro), grad, jnp.zeros_like(grad))
    if last:
        grad = jnp.where(is_last, last[0][step], grad)
    grad_ref[...] = grad
    rows = jnp.dot(turned_ref[pick], grad, preferred_element_type=F32)
    for j in range(rows_ref.shape[0]):
        rows_ref[j] = rows[j * cap : (j + 1) * cap].astype(BF16)


def run_rows(step, turned, incoming, last_grad, experts, cap):
    last = [last_grad] if step < last_grad.shape[0] else []
    return pl.pallas_call(
        functools.partial(rows_kernel, step=step, cap=cap),
        in_specs=whole(pltpu.VMEM, 2 + len(last)),
        out_specs=whole(pltpu.VMEM, 2),
        out_shape=[
            jax.ShapeDtypeStruct(incoming.shape, BF16),
            jax.ShapeDtypeStruct((experts, cap, incoming.shape[1]), BF16),
        ],
        compiler_params=pltpu.CompilerParams(vmem_limit_bytes=4 * MIB),
        name="rows",
    )(turned, incoming, *last)


def finish_kernel(*refs, scale):
    *part_refs, gain_ref, router_ref = refs
    total = part_refs[0][...]
    for part_ref in part_refs[1:]:
        total = total + part_ref[...]
    total = total * scale
    gain_ref[...] = total[:1]
    router_ref[...] = total[1:]


def run_finish(parts, scale):
    rows, width = parts[0].shape
    return pl.pallas_call(
        functools.partial(finish_kernel, scale=scale),
        in_specs=whole(pltpu.VMEM, len(parts)),
        out_specs=whole(pltpu.VMEM, 2),
        out_shape=[
            jax.ShapeDtypeStruct((1, width), F32),
            jax.ShapeDtypeStruct((rows - 1, width), F32),
        ],
        compiler_params=pltpu.CompilerParams(vmem_limit_bytes=4 * MIB),
        name="finish",
    )(*parts)


def per_device(acts, out_grad, ln_gain, router, w_in, w_out, expert_ids, slot_ids, capacity):
    sections = lax.axis_size("section")
    cores = lax.axis_size("dp")
    micro = acts.shape[1]
    tokens = acts.shape[2]
    width = acts.shape[3]
    experts = router.shape[2]
    top = expert_ids.shape[3]
    cap = 5 * tokens * top // (4 * experts)
    all_tokens = tokens * lax.axis_size("expert") * cores
    scale = 1.0 / math.sqrt(micro * all_tokens)
    tile = min(1024, w_in.shape[3])
    acts, caps, gain = acts[0], capacity[0], ln_gain
    ids, places = jnp.swapaxes(expert_ids[0], 1, 2), jnp.swapaxes(slot_ids[0], 1, 2)
    inputs = (acts, gain, router[0].T, ids, places, caps[:, None, :])

    def both_halves(own):
        turns = [[(i, (i + by) % cores) for i in range(cores)] for by in range(1, cores)]
        return [own] + [lax.ppermute(own, "dp", pairs) for pairs in turns]

    first_parts = both_halves(w_in[0, 0])
    second_parts = both_halves(w_out[0, 0])

    sent, turned0, router_pad = run_prepare(inputs, out_grad, [], (0,), cap)
    packed0 = jnp.concatenate(exchange([sent[j, 0] for j in range(experts)]), axis=0)
    split = width + LANES
    u0, grad_rows = packed0[None, :, :split], packed0[:, split:]
    rest, turned, _, sel, first_own, second_own = run_prepare(
        inputs, None, [w_in[0, 0], w_out[0, 0]], tuple(range(1, micro)), cap
    )
    first_parts[0], second_parts[0] = first_own, second_own
    own_turned = [run_turn(part) for part in (first_own, second_own)]
    others, _ = lax.optimization_barrier((first_parts[1:] + second_parts[1:], own_turned))
    others = [run_turn(part) for part in others]
    first_turned = own_turned[:1] + others[: cores - 1]
    second_turned = own_turned[1:] + others[cores - 1 :]
    turned = jnp.concatenate([turned0, turned], axis=0)

    rows_u = u0
    sums = []
    grad = out_grad[0]
    steps = micro + sections - 1
    results = []
    down = [(i, i - 1) for i in range(1, sections)]
    swap = [(sections - 1 - i, sections - 1 - (i ^ 1)) for i in range(sections)]
    for step in range(steps):
        if step > 0:
            rows_u = stack
            single = sections % 2 == 0 and step in (1, steps - 1)
            ring = down + [(0, sections - 1)]
            chain = ring if step >= micro else down
            incoming = lax.ppermute(results[-1], "section", swap if single else chain)
            grad, sent = run_rows(step, turned, incoming, out_grad, experts, cap)
            grad_rows = jnp.concatenate(exchange([sent[j] for j in range(experts)]), axis=0)
        active, slope = run_hidden(step, rows_u, first_parts, tile)
        slot_rows, shared = run_experts(
            step, rows_u, grad_rows, active, slope,
            first_turned if step else own_turned[:1] + first_parts[1:],
            second_turned if step else own_turned[1:] + second_parts[1:],
            router_pad, gain, sums, experts, tile, [NN] + [NN if step else NT] * (cores - 1),
        )
        sums = [shared]
        chunks = [slot_rows[j * cap : (j + 1) * cap] for j in range(experts)]
        if step == steps - 1:
            tail = jnp.concatenate([shared[:1], shared[8 : 8 + experts]], axis=0).astype(BF16)
            tail = jnp.pad(tail, ((0, -(cap + 1 + experts) % 16), (0, 0)))
            chunks = [jnp.concatenate([chunk, tail], axis=0) for chunk in chunks]
        back = exchange(chunks, back=True)
        if step == 0:
            rest, _ = lax.optimization_barrier((rest, back[-1]))
            rest = exchange([rest[j] for j in range(experts)])
            stack = jnp.concatenate([u0, jnp.concatenate(rest, axis=1)], axis=0)
        ret = jnp.concatenate([chunk[:cap] for chunk in back], axis=0)
        earlier = results if step == steps - 1 else []
        results.append(run_tokens(step, acts, gain, sel, ret, grad, earlier))

    total = sum(chunk[cap : cap + 1 + experts].astype(F32) for chunk in back)
    parts = [total]
    for by in range(1, cores):
        parts.append(lax.ppermute(total, "dp", [(i, (i + by) % cores) for i in range(cores)]))
    gain_grad, router_grad = run_finish(parts, scale)
    return (results[-1][None], gain_grad, router_grad.T[None])


def solution(mesh):
    return jax.shard_map(
        per_device,
        mesh=mesh,
        in_specs=(
            P("section", None, ("expert", "dp"), None),
            P(None, ("expert", "dp"), None),
            P("section", None),
            P("section", None, None),
            P("section", "expert", None, "dp"),
            P("section", "expert", "dp", None),
            P("section", None, ("expert", "dp"), None),
            P("section", None, ("expert", "dp"), None),
            P("section", None, None),
        ),
        out_specs=(
            P("section", None, ("expert", "dp"), None),
            P("section", None),
            P("section", None, None),
        ),
        check_vma=False,
    )
```
